32 devices in a mesh: fsdp: 8 (over z, x), head: 4 (over y, core).
Axes of the slice: x: 2, y: 2, z: 4, core: 2. Of those that a mesh axis runs over, the one named last changes fastest.
Arguments:
- block_in: bfloat16 [16384, 1024], P('fsdp', 'head'), may hold values from -6 to 6
- segment_ids: int32 [16, 1024], P('fsdp'), may hold values from 0 to 3, never falling along the last dimension, each value on 1 to 512 neighbouring positions
- norm_gain: float32 [1024], replicated, may hold values from 0.1 to 1.9
- proj_z: bfloat16 [1024, 2048], P('fsdp', 'head'), may hold values from -0.1875 to 0.1875
- proj_x: bfloat16 [1024, 2048], P('fsdp', 'head'), may hold values from -0.1875 to 0.1875
- proj_bc: bfloat16 [1024, 256], P('fsdp'), may hold values from -0.1875 to 0.1875
- proj_dt: bfloat16 [1024, 32], P('fsdp', 'head'), may hold values from -0.1875 to 0.1875
- conv_x: float32 [4, 2048], P(None, 'head'), may hold values from -0.5 to 0.5
- bias_x: float32 [2048], P('head'), may hold values from -1.2 to 1.2
- conv_bc: float32 [4, 256], replicated, may hold values from -0.5 to 0.5
- bias_bc: float32 [256], replicated, may hold values from -1.2 to 1.2
- dt_bias: float32 [32], P('head'), may hold values from -7 to -2.5
- a_log: float32 [32], P('head'), may hold values from 0 to 2.77
- skip_d: float32 [32], P('head'), may hold values from 0.5 to 1.5
- gate_gain: float32 [2048], P('head'), may hold values from 0.1 to 1.9
- proj_out: bfloat16 [2048, 1024], P('head', 'fsdp'), may hold values from -0.125 to 0.125
- cotangent: bfloat16 [16384, 1024], P('fsdp', 'head'), may hold values from -6 to 6
Outputs:
- block_out: bfloat16 [16384, 1024], P('fsdp', 'head')
- grad_block_in: bfloat16 [16384, 1024], P('fsdp', 'head')
- grad_norm_gain: float32 [1024], P('head')
- grad_proj_z: float32 [1024, 2048], P('fsdp', 'head')
- grad_proj_x: float32 [1024, 2048], P('fsdp', 'head')
- grad_proj_bc: float32 [1024, 256], P('fsdp', 'head')
- grad_proj_dt: float32 [1024, 32], P('fsdp', 'head')
- grad_conv_x: float32 [4, 2048], P(None, 'head')
- grad_bias_x: float32 [2048], P('head')
- grad_conv_bc: float32 [4, 256], replicated
- grad_bias_bc: float32 [256], replicated
- grad_dt_bias: float32 [32], P('head')
- grad_a_log: float32 [32], P('head')
- grad_skip_d: float32 [32], P('head')
- grad_gate_gain: float32 [2048], P('head')
- grad_proj_out: float32 [2048, 1024], P('head', 'fsdp')
The draws below stay inside these ranges and needn't reach their ends.
Inputs may be any that keep to these rules, and one draw needn't show every extreme that they name: `segment_ids`: segment numbers never fall along a sequence; tokens of one sequence with equal numbers form one document.
All inputs are finite; a program needn't handle non-finite values.
Results may differ from the reference program's by a relative error of at most 0.011.
Values may be sent and summed in bfloat16 or wider, within the bound.
No kernel may reach another device: no remote copies, remote signals or barrier semaphores. Data moves between devices by JAX's collectives and lax.ppermute only.
A program may use at most 128 MiB of HBM per device.

```python
import math
import jax
import jax.numpy as jnp
import numpy as np
from jax import lax

D = 1024
H = 32
P_SIZE = 64
DS = 128
CONV = 4
SEQ_LEN = 1024
GROUP = 256
DI = 2048
SEQS = 16
TOKENS = 16384


def levels(key, extent, split, low, largest):
    loudness, own = 1.0, jax.random.fold_in(key, 6)
    for position, shards_of in split:
        draws = jnp.exp(jax.random.uniform(jax.random.fold_in(own, position), (shards_of,), jnp.float32, low / len(split), largest / len(split)))
        loudness = loudness * jnp.repeat(draws, extent[position] // shards_of).reshape([-1 if axis == position else 1 for axis in range(len(extent))])
    return loudness


def profile(number_of, total, limit, skew):
    loads = [(1 << 20) // math.isqrt(standing ** skew) + 1 for standing in range(2, number_of + 1)]
    spare, given = total - limit - (number_of - 1), [1] * (number_of - 1)
    while spare > 0:
        movable = [i for i in range(number_of - 1) if given[i] < limit]
        whole, budget = sum([loads[i] for i in movable]), spare
        for i in movable:
            extra = min(limit - given[i], max(1, budget * loads[i] // whole), spare)
            given[i] = given[i] + extra
            spare = spare - extra
    return np.array([limit] + given)


def ragged(own_key, count, total, bound, skew):
    if count == 2:
        one = jax.random.randint(own_key, (), max(1, total - bound), min(bound, total - 1) + 1)
        return jnp.stack([one, total - one])
    lengths = jnp.asarray(profile(count, total, bound, skew), jnp.int32)
    couples = (count - 1) // 2
    giver, sink = lengths[1:1 + 2 * couples:2], lengths[2:2 + 2 * couples:2]
    room = jnp.minimum(giver - 1, bound - sink)
    shifted = jax.random.randint(jax.random.fold_in(own_key, 1), (couples,), 0, 1 << 20) % (room + 1)
    lengths = lengths.at[1:1 + 2 * couples:2].set(giver - shifted).at[2:2 + 2 * couples:2].set(sink + shifted)
    return lengths[jax.random.permutation(jax.random.fold_in(own_key, 2), count)]


def normal_values(key, extent, width, limit, split=(), kind=jnp.bfloat16):
    gain = levels(key, extent, split, -0.22, 0.18) if split else 1.0
    entries = jax.random.normal(key, extent, jnp.float32) * width * gain
    return jnp.minimum(jnp.maximum(entries, -limit), limit).astype(kind)


def setup_inputs(seed: int = 0) -> dict:
    seeds = jax.random.split(jax.random.key(seed), 18)
    block_in = normal_values(seeds[0], (TOKENS, D), 1.0, 6.0, ((0, 8), (1, 4)))
    segment_ids = jax.vmap(lambda own: jnp.searchsorted(jnp.cumsum(ragged(own, 4, SEQ_LEN, SEQ_LEN // 2, 0)), jnp.arange(SEQ_LEN), side="right"))(jax.random.split(seeds[1], SEQS)).reshape((SEQS, SEQ_LEN)).astype(jnp.int32)
    norm_gain = jnp.clip(1.0 + 0.18 * jax.random.normal(seeds[2], (D,), jnp.float32), 0.1, 1.9)
    proj_z = normal_values(seeds[3], (D, DI), D ** -0.5, 0.1875, ((0, 8), (1, 4)))
    proj_x = normal_values(seeds[4], (D, DI), D ** -0.5, 0.1875, ((0, 8), (1, 4)))
    proj_bc = normal_values(seeds[5], (D, 2 * DS), D ** -0.5, 0.1875, ((0, 8),))
    proj_dt = normal_values(seeds[6], (D, H), D ** -0.5, 0.1875, ((0, 8), (1, 4)))
    conv_x = jnp.clip(jax.random.uniform(seeds[7], (CONV, DI), jnp.float32, -0.5, 0.5) * levels(seeds[7], (CONV, DI), ((1, 4),), -0.4, 0.0), -0.5, 0.5)
    bias_x = normal_values(seeds[8], (DI,), 0.3, 1.2, ((0, 4),), jnp.float32)
    conv_bc = jnp.clip(jax.random.uniform(seeds[9], (CONV, 2 * DS), jnp.float32, -0.5, 0.5), -0.5, 0.5)
    bias_bc = normal_values(seeds[10], (2 * DS,), 0.3, 1.2, (), jnp.float32)
    dt_bias = jnp.clip(-7.0 + 4.5 * jax.random.uniform(seeds[11], (H,), jnp.float32) ** levels(seeds[11], (H,), ((0, 4),), -0.2, 0.2), -7.0, -2.5)
    a_log = jnp.clip(2.77 * jax.random.uniform(seeds[12], (H,), jnp.float32) ** levels(seeds[12], (H,), ((0, 4),), -0.2, 0.2), 0.0, 2.77)
    skip_d = jnp.clip(0.5 + 1.0 * jax.random.uniform(seeds[13], (H,), jnp.float32) ** levels(seeds[13], (H,), ((0, 4),), -0.2, 0.2), 0.5, 1.5)
    gate_gain = jnp.clip(1.0 + 0.18 * jax.random.normal(seeds[14], (DI,), jnp.float32), 0.1, 1.9)
    proj_out = normal_values(seeds[15], (DI, D), DI ** -0.5, 0.125, ((0, 4), (1, 8)))
    cotangent = normal_values(seeds[16], (TOKENS, D), 1.0, 6.0, ((0, 8), (1, 4)))
    return dict(block_in=block_in, segment_ids=segment_ids, norm_gain=norm_gain, proj_z=proj_z, proj_x=proj_x, proj_bc=proj_bc, proj_dt=proj_dt, conv_x=conv_x, bias_x=bias_x, conv_bc=conv_bc, bias_bc=bias_bc, dt_bias=dt_bias, a_log=a_log, skip_d=skip_d, gate_gain=gate_gain, proj_out=proj_out, cotangent=cotangent)


epsilon = 1e-05
neg_big = -1e+30

@jax.custom_vjp
def low(v):
    return lax.optimization_barrier(v.astype(jnp.bfloat16)).astype(jnp.float32)

@jax.custom_vjp
def low_back(v):
    return v

def low_keep(v):
    return (low(v), None)

def low_pass(kept, grad):
    return (grad,)

def back_keep(v):
    return (v, None)

def back_low(kept, grad):
    return (low(grad),)
low.defvjp(low_keep, low_pass)
low_back.defvjp(back_keep, back_low)

def matmul_high(left_side, right_side):
    return jnp.dot(left_side, right_side, precision=lax.Precision.HIGHEST)

def shift_down(values, shift_by):
    if shift_by == 0:
        return values
    padding = jnp.zeros((shift_by,) + values.shape[1:], values.dtype)
    return jnp.concatenate([padding, values[:-shift_by]], 0)

def conv_masks(segment, tap_count):
    mask_list = []
    for shift_by in range(tap_count):
        if shift_by == 0:
            mask_list.append(jnp.ones(segment.shape, jnp.float32))
        else:
            earlier = jnp.concatenate([jnp.full((shift_by,), -1, jnp.int32), segment[:-shift_by].astype(jnp.int32)], 0)
            mask_list.append((earlier == segment.astype(jnp.int32)).astype(jnp.float32))
    return mask_list

def conv_fwd(inputs, weight, conv_bias, mask_list):
    tap_count = weight.shape[0]
    summed = jnp.broadcast_to(conv_bias[None, :], inputs.shape)
    for tap_index in range(tap_count):
        shift_by = tap_count - 1 - tap_index
        summed = summed + weight[tap_index][None, :] * shift_down(inputs, shift_by) * mask_list[shift_by][:, None]
    return summed

def block_forward(params, rows, segment):
    norm_gain, proj_z, proj_x, proj_bc, proj_dt, conv_x, bias_x, conv_bc, bias_bc, dt_bias, a_log, skip_d, gate_gain, proj_out = params
    high = lax.Precision.HIGHEST
    norm_rs = lax.rsqrt(lax.optimization_barrier(jnp.mean(rows * rows, -1, keepdims=True)) + epsilon)
    hidden = low(rows * norm_rs * norm_gain[None, :])
    gate_pre = low_back(matmul_high(hidden, proj_z))
    x_pre = low_back(matmul_high(hidden, proj_x))
    bc_pre = low_back(matmul_high(hidden, proj_bc))
    dt_raw = low_back(matmul_high(hidden, proj_dt))
    mask_list = conv_masks(segment, CONV)
    x_low = low(jax.nn.silu(conv_fwd(x_pre, conv_x, bias_x, mask_list)))
    bc_low = low(jax.nn.silu(conv_fwd(bc_pre, conv_bc, bias_bc, mask_list)))
    n_groups = SEQ_LEN // GROUP
    b_groups = bc_low[:, :DS].reshape(n_groups, GROUP, DS)
    c_groups = bc_low[:, DS:].reshape(n_groups, GROUP, DS)
    seg_groups = segment.astype(jnp.int32).reshape(n_groups, GROUP)
    gram = jnp.einsum('cqn,csn->cqs', c_groups, b_groups, precision=high)
    step_dt = jax.nn.softplus(dt_raw + dt_bias[None, :])
    rate = -jnp.exp(a_log)
    cumul = jnp.cumsum(step_dt * rate[None, :], 0)
    local_pos = jnp.arange(GROUP)
    allowed = (local_pos[None, :] <= local_pos[:, None])[None] & (seg_groups[:, None, :] == seg_groups[:, :, None])
    end_seg = seg_groups[:, -1]
    prev_seg = jnp.concatenate([jnp.full((1,), -1, jnp.int32), end_seg[:-1]], 0)
    x_heads = x_low.reshape(SEQ_LEN, H, P_SIZE).transpose(1, 0, 2)
    x_groups = x_heads.reshape(H, n_groups, GROUP, P_SIZE)
    cum_groups = cumul.T.reshape(H, n_groups, GROUP)
    dt_groups = step_dt.T.reshape(H, n_groups, GROUP)

    def head_mix(item):
        x_head, cum_head, dt_head = item
        decay = jnp.exp(jnp.where(allowed, cum_head[:, :, None] - cum_head[:, None, :], neg_big))
        mix = low(gram * decay * dt_head[:, None, :])
        intra = jnp.einsum('cqs,csp->cqp', mix, x_head, precision=high)
        end_cum = cum_head[:, -1]
        prev_cum = jnp.concatenate([jnp.zeros((1,), end_cum.dtype), end_cum[:-1]], 0)
        w_end = jnp.exp(jnp.where(seg_groups == end_seg[:, None], end_cum[:, None] - cum_head, neg_big)) * dt_head
        state = jnp.einsum('csn,cs,csp->cnp', b_groups, w_end, x_head, precision=high)
        carry_gain = jnp.exp(jnp.where(end_seg == prev_seg, end_cum - prev_cum, neg_big))
        held = jnp.zeros((DS, P_SIZE), state.dtype)
        entering_list = []
        for group_index in range(n_groups):
            entering_list.append(held)
            held = state[group_index] + carry_gain[group_index] * held
        entering = jnp.stack(entering_list, 0)
        a_in = jnp.exp(jnp.where(seg_groups == prev_seg[:, None], cum_head - prev_cum[:, None], neg_big))
        inter = a_in[:, :, None] * jnp.einsum('cqn,cnp->cqp', c_groups, entering, precision=high)
        return intra + inter
    mixed = lax.map(jax.checkpoint(head_mix), (x_groups, cum_groups, dt_groups)).reshape(H, SEQ_LEN, P_SIZE)
    y_heads = mixed + skip_d[:, None, None] * x_heads
    y_flat = low_back(y_heads.transpose(1, 0, 2).reshape(SEQ_LEN, H * P_SIZE))
    gated = y_flat * jax.nn.silu(gate_pre)
    gate_rs = lax.rsqrt(lax.optimization_barrier(jnp.mean(gated * gated, -1, keepdims=True)) + epsilon)
    out_low = low(gated * gate_rs * gate_gain[None, :])
    return rows + matmul_high(out_low, proj_out)

def reference(block_in, segment_ids, norm_gain, proj_z, proj_x, proj_bc, proj_dt, conv_x, bias_x, conv_bc, bias_bc, dt_bias, a_log, skip_d, gate_gain, proj_out, cotangent):
    params = tuple((param.astype(jnp.float32) for param in (norm_gain, proj_z, proj_x, proj_bc, proj_dt, conv_x, bias_x, conv_bc, bias_bc, dt_bias, a_log, skip_d, gate_gain, proj_out)))
    rows_all = block_in.astype(jnp.float32).reshape(SEQS, SEQ_LEN, D)
    cot_all = cotangent.astype(jnp.float32).reshape(SEQS, SEQ_LEN, D)

    def per_sequence(totals, item):
        rows, cot_rows, segment = item
        result, pullback = jax.vjp(lambda weights, inputs: block_forward(weights, inputs, segment), params, rows)
        grad_weights, grad_rows = pullback(cot_rows)
        totals = jax.tree.map(lambda summed_grad, new_grad: summed_grad + new_grad, totals, grad_weights)
        return (totals, (result.astype(jnp.bfloat16), grad_rows.astype(jnp.bfloat16)))
    start = jax.tree.map(jnp.zeros_like, params)
    totals, (outputs, grads) = lax.scan(per_sequence, start, (rows_all, cot_all, segment_ids))
    return (outputs.reshape(TOKENS, D), grads.reshape(TOKENS, D), totals[0], totals[1], totals[2], totals[3], totals[4], totals[5], totals[6], totals[7], totals[8], totals[9], totals[10], totals[11], totals[12], totals[13])
```

```python
import functools

import jax
import jax.numpy as jnp
from jax import lax
from jax.experimental import pallas as pl
from jax.experimental.pallas import tpu as pltpu
from jax.sharding import PartitionSpec as P

GROUP = 256
LANE = 128
SUB = 8

epsilon = 1e-05
neg_big = -1e30
f32 = jnp.float32
bf16 = jnp.bfloat16

VMEM_LIMIT = 56 * 1024 * 1024


def dot(left, right, left_dim=1, right_dim=0):
    return lax.dot_general(
        left, right, (((left_dim,), (right_dim,)), ((), ())), preferred_element_type=f32
    )


def sigmoid(values):
    return 1.0 / (1.0 + jnp.exp(-values))


def softplus(values):
    return jnp.maximum(values, 0.0) + jnp.log1p(jnp.exp(-jnp.abs(values)))


def split_pack(values, count):
    high = values.astype(bf16).astype(f32)
    rest = values - high
    mid = rest.astype(bf16).astype(f32)
    last = rest - mid
    packed = high + pltpu.roll(mid, count, 1) + pltpu.roll(last, 2 * count, 1)
    return packed.astype(bf16)


def fold_lanes(values, count):
    lanes = values.shape[1]
    return values + pltpu.roll(values, lanes - count, 1) + pltpu.roll(values, lanes - 2 * count, 1)


def triangle(size, upper):
    row = lax.broadcasted_iota(jnp.int32, (size, size), 0)
    col = lax.broadcasted_iota(jnp.int32, (size, size), 1)
    return (row <= col if upper else row >= col)


def head_sums(values, heads_of):
    high = values.astype(bf16)
    low = (values - high.astype(f32)).astype(bf16)
    return dot(high, heads_of) + dot(low, heads_of)


def to_rows(column):
    wide = jnp.broadcast_to(column, (column.shape[0], LANE))
    return wide.T[:SUB]


def to_column(rows):
    return rows.T[:, :1]


def block_slice(index):
    return pl.ds(pl.multiple_of(index * LANE, LANE), LANE)


def forward_kernel(
    heads, head_dim, state_dim,
    meta, link, row0, row1, row2, row3, tok, seg_row, w, gain, taps, head_par, chan, spread,
    hid, xb_pre, xb_conv, z_out, v_out, cum_out, y_out, enter_out, sq_out, rs_out,
    ext, held,
):
    inner = heads * head_dim
    mixed = inner + 2 * state_dim
    step = pl.program_id(0)
    me = meta[0]
    parts = [ref[...].astype(f32) for ref in (row0, row1, row2, row3)]
    total = sum([jnp.sum(part * part, -1, keepdims=True) for part in parts])
    width = 4 * parts[0].shape[1]
    rs = lax.rsqrt(total / width + epsilon)
    rs_out[0] = to_rows(rs)
    per = parts[0].shape[1] // LANE
    for rel in range(4):
        absolute = jnp.bitwise_xor(me, rel)
        for half in range(per):
            feature = absolute * per + half
            scale = gain[:, block_slice(feature)]
            part = parts[rel][:, half * LANE:(half + 1) * LANE]
            hid[:, block_slice(meta[1 + feature])] = (part * rs * scale).astype(bf16)
    hidden = hid[...]

    @pl.when(step == 0)
    def _():
        ext[0:SUB] = jnp.zeros((SUB, mixed), f32)
        held[...] = jnp.zeros(held.shape, f32)

    @pl.when(step > 0)
    def _():
        ext[0:SUB] = ext[GROUP:GROUP + SUB]

    pre = dot(hidden, w[:, :mixed])
    ext[SUB:SUB + GROUP] = pre
    xb_pre[...] = pre
    z = dot(hidden, w[:, mixed:mixed + inner])
    z_out[...] = z
    masks = [None] + [jnp.broadcast_to(tok[:, k:k + 1], (GROUP, LANE)) for k in (1, 2, 3)]
    acts = []
    for start in range(0, mixed, LANE):
        cols = slice(start, start + LANE)
        conv = taps[4:5, cols] + taps[3:4, cols] * ext[SUB:SUB + GROUP, cols]
        for k in (1, 2, 3):
            conv = conv + taps[3 - k:4 - k, cols] * (ext[SUB - k:SUB - k + GROUP, cols] * masks[k])
        xb_conv[:, cols] = conv
        acts.append((conv * sigmoid(conv)).astype(bf16))
    x = jnp.concatenate(acts[:inner // LANE], 1)
    b = jnp.concatenate(acts[inner // LANE:(inner + state_dim) // LANE], 1)
    c = jnp.concatenate(acts[(inner + state_dim) // LANE:], 1)

    lane = lax.broadcasted_iota(jnp.int32, (GROUP, LANE), 1)
    real = lane < heads
    v = dot(hidden, w[:, mixed + inner:]) + head_par[0:1]
    v_out[...] = v
    dt = jnp.where(real, softplus(v), 0.0)
    tri = triangle(GROUP, False)
    tri_low = tri.astype(f32).astype(bf16)
    cum = fold_lanes(dot(tri_low, split_pack(dt * head_par[1:2], heads)), heads)
    cum = jnp.where(real, cum, 0.0)
    cum_out[...] = cum
    cum_t = cum.T
    end = cum[GROUP - 1:GROUP]
    ain = jnp.where(real, jnp.exp(cum) * tok[:, 5:6], 0.0)
    w_end = jnp.where(real, jnp.exp(end - cum) * tok[:, 4:5], 0.0)
    carry = jnp.where(real[:SUB], jnp.exp(jnp.broadcast_to(end, (SUB, LANE))) * link[step], 0.0)
    wide = dot(
        jnp.concatenate([split_pack(a, heads) for a in (dt, ain, w_end)], 0), spread[...]
    )
    dt_wide, ain_wide, end_wide = wide[:GROUP], wide[GROUP:2 * GROUP], wide[2 * GROUP:]
    carry_wide = dot(split_pack(carry, heads), spread[...])[0:1]
    x32 = x.astype(f32)
    xdt32 = x32 * dt_wide
    xdt = xdt32.astype(bf16)
    xw = (xdt32 * end_wide).astype(bf16)

    gram = dot(c, b, 1, 1)
    allowed = tri & (tok[:, 0:1] == seg_row[0])
    off = jnp.where(allowed, 0.0, neg_big)
    first = lax.broadcasted_iota(jnp.int32, (GROUP, LANE), 1) < head_dim
    entering = held[...]
    enter_out[0] = entering
    u = dot(c, entering.astype(bf16))
    gated_sq = jnp.zeros((GROUP, LANE), f32)
    zero = jnp.zeros((GROUP, LANE), bf16)
    for pair in range(heads // 2):
        cols = slice(pair * LANE, (pair + 1) * LANE)
        xp = xdt[:, cols]
        intra = 0.0
        for odd in range(2):
            head = 2 * pair + odd
            decay = jnp.exp(cum[:, head:head + 1] - cum_t[head:head + 1] + off)
            weight = (gram * decay).astype(bf16)
            mine = jnp.where(first, xp, zero) if odd == 0 else jnp.where(first, zero, xp)
            intra = intra + dot(weight, mine)
        y = intra + ain_wide[:, cols] * u[:, cols] + chan[0:1, cols] * x32[:, cols]
        y_out[:, cols] = y
        zc = z[:, cols]
        gated = y * zc * sigmoid(zc)
        gated_sq = gated_sq + gated * gated
    held[...] = dot(b, xw, 0, 0) + carry_wide * entering
    sq_out[0] = to_rows(jnp.sum(gated_sq, -1, keepdims=True))


def gate_kernel(
    inner_full,
    meta, sq0, sq1, sq2, sq3, z, y, cot0, cot1, cot2, cot3, w_out, chan,
    out0, out1, out2, out3, yn_out, dyn_out, cot_out, gd_out, gain_out,
):
    step = pl.program_id(0)
    me = meta[0]
    square = to_column(sq0[0] + sq1[0] + sq2[0] + sq3[0])
    rs = lax.rsqrt(square / inner_full + epsilon)
    inner = z.shape[1]
    strips = [slice(s, s + LANE) for s in range(0, inner, LANE)]
    norms, gates = [], []
    for cols in strips:
        zc = z[:, cols]
        gated = y[:, cols] * zc * sigmoid(zc)
        gnorm = gated * rs
        gates.append(gated)
        norms.append(gnorm)
        yn_out[:, cols] = (gnorm * chan[1:2, cols]).astype(bf16)
    yn = yn_out[...]
    per = cot0.shape[1] // LANE
    dyn = 0.0
    for rel, (cot, out) in enumerate(((cot0, out0), (cot1, out1), (cot2, out2), (cot3, out3))):
        absolute = jnp.bitwise_xor(me, rel)
        places = [meta[1 + absolute * per + half] for half in range(per)]
        weight = jnp.concatenate([w_out[place] for place in places], 1)
        out[...] = dot(yn, weight).astype(bf16)
        cv = cot[...]
        dyn = dyn + dot(cv, weight, 1, 1)
        for half, place in enumerate(places):
            cot_out[:, block_slice(place)] = cv[:, half * LANE:(half + 1) * LANE]
    dyn_out[...] = dyn

    @pl.when(step == 0)
    def _():
        gain_out[...] = jnp.zeros(gain_out.shape, f32)

    gd = jnp.zeros((GROUP, LANE), f32)
    for index, cols in enumerate(strips):
        dc = dyn[:, cols]
        gd = gd + dc * chan[1:2, cols] * gates[index]
        gain_out[0:1, cols] += jnp.sum(dc * norms[index], 0, keepdims=True)
    gd_out[0] = to_rows(jnp.sum(gd, -1, keepdims=True))


def backward_kernel(
    heads, head_dim, state_dim, inner_full, n_groups,
    meta, link, sq0, sq1, sq2, sq3, gd0, gd1, gd2, gd3, z, y, dyn, xb_pre, xb_conv, v_in, cum_in,
    enter_in, tok, seg_row, hid, w, taps, head_par, chan, spread, heads_of,
    dcat, dh0, dh1, dh2, dh3, nd_out, conv_out, head_out, skip_out,
    ext1, ext2, ext3, dheld,
):
    inner = heads * head_dim
    mixed = inner + 2 * state_dim
    step = pl.program_id(0)
    group = n_groups - 1 - step
    me = meta[0]

    @pl.when(step == 0)
    def _():
        for ext in (ext1, ext2, ext3):
            ext[GROUP:GROUP + SUB] = jnp.zeros((SUB, mixed), f32)
        dheld[...] = jnp.zeros(dheld.shape, f32)
        conv_out[...] = jnp.zeros(conv_out.shape, f32)
        head_out[...] = jnp.zeros(head_out.shape, f32)
        skip_out[...] = jnp.zeros(skip_out.shape, f32)

    @pl.when(step > 0)
    def _():
        for ext in (ext1, ext2, ext3):
            ext[GROUP:GROUP + SUB] = ext[0:SUB]

    square = to_column(sq0[0] + sq1[0] + sq2[0] + sq3[0])
    rs = lax.rsqrt(square / inner_full + epsilon)
    inner_dot = to_column(gd0[0] + gd1[0] + gd2[0] + gd3[0]) * rs / inner_full
    dys = []
    for start in range(0, inner, LANE):
        cols = slice(start, start + LANE)
        zc, yc = z[:, cols], y[:, cols]
        sg = sigmoid(zc)
        zs = zc * sg
        gnorm = yc * zs * rs
        dgated = rs * (dyn[:, cols] * chan[1:2, cols] - gnorm * inner_dot)
        dys.append((dgated * zs).astype(bf16))
        dz = dgated * yc * (sg * (1.0 + zc * (1.0 - sg)))
        dcat[:, mixed + start:mixed + start + LANE] = dz.astype(bf16)
    dy = jnp.concatenate(dys, 1)
    dy32 = dy.astype(f32)

    acts, slopes = [], []
    for start in range(0, mixed, LANE):
        conv = xb_conv[:, start:start + LANE]
        sg = sigmoid(conv)
        acts.append((conv * sg).astype(bf16))
        slopes.append(sg * (1.0 + conv * (1.0 - sg)))
    x = jnp.concatenate(acts[:inner // LANE], 1)
    b = jnp.concatenate(acts[inner // LANE:(inner + state_dim) // LANE], 1)
    c = jnp.concatenate(acts[(inner + state_dim) // LANE:], 1)
    x32 = x.astype(f32)

    lane = lax.broadcasted_iota(jnp.int32, (GROUP, LANE), 1)
    real = lane < heads
    v = v_in[...]
    dt = jnp.where(real, softplus(v), 0.0)
    cum = cum_in[...]
    cum_t = cum.T
    end = cum[GROUP - 1:GROUP]
    ain = jnp.where(real, jnp.exp(cum) * tok[:, 5:6], 0.0)
    w_end = jnp.where(real, jnp.exp(end - cum) * tok[:, 4:5], 0.0)
    carry = jnp.where(real[:SUB], jnp.exp(jnp.broadcast_to(end, (SUB, LANE))) * link[group], 0.0)
    wide = dot(
        jnp.concatenate([split_pack(a, heads) for a in (dt, ain, w_end)], 0), spread[...]
    )
    dt_wide, ain_wide, end_wide = wide[:GROUP], wide[GROUP:2 * GROUP], wide[2 * GROUP:]
    carry_wide = dot(split_pack(carry, heads), spread[...])[0:1]
    xdt32 = x32 * dt_wide
    xdt = xdt32.astype(bf16)
    xw = (xdt32 * end_wide).astype(bf16)

    entering = enter_in[0]
    enter_low = entering.astype(bf16)
    dstate = dheld[...]
    dstate_low = dstate.astype(bf16)
    dyw = (dy32 * ain_wide).astype(bf16)
    dc = dot(dyw, enter_low, 1, 1)
    db = dot(xw, dstate_low, 1, 1)
    bd = dot(b, dstate_low)
    gain_sum = jnp.sum(dstate * entering, 0, keepdims=True) * carry_wide
    dheld[...] = dot(c, dyw, 0, 0) + carry_wide * dstate

    gram_t = dot(b, c, 1, 1)
    tri_up = triangle(GROUP, True)
    off = jnp.where(tri_up & (tok[:, 0:1] == seg_row[0]), 0.0, neg_big)
    first = lane < head_dim
    zero = jnp.zeros((GROUP, LANE), bf16)
    dgram_t = jnp.zeros((GROUP, GROUP), f32)
    flow, through = [], []
    for pair in range(heads // 2):
        cols = slice(pair * LANE, (pair + 1) * LANE)
        xp, dyp = xdt[:, cols], dy[:, cols]
        dxw = 0.0
        for odd in range(2):
            head = 2 * pair + odd
            decay = jnp.exp(cum_t[head:head + 1] - cum[:, head:head + 1] + off)
            weight = (gram_t * decay).astype(bf16)
            own_dy = jnp.where(first, dyp, zero) if odd == 0 else jnp.where(first, zero, dyp)
            own_x = jnp.where(first, xp, zero) if odd == 0 else jnp.where(first, zero, xp)
            dxw = dxw + dot(weight, own_dy)
            dgram_t = dgram_t + dot(own_x, dyp, 1, 1) * decay
        x_cols, dy_cols = x32[:, cols], dy32[:, cols]
        ymix = y[:, cols] - chan[0:1, cols] * x_cols
        flow.append(dy_cols * ymix - xp.astype(f32) * dxw)
        through.append(dxw + end_wide[:, cols] * bd[:, cols])
        skip_out[0:1, cols] += jnp.sum(dy_cols * x_cols, 0, keepdims=True)
    dgram_low = dgram_t.astype(bf16)
    db = db + dot(dgram_low, c)
    dc = dc + dot(dgram_low, b, 0, 0)
    q = jnp.concatenate(through, 1)
    flow_sum = head_sums(jnp.concatenate(flow, 1), heads_of[...])
    ddt = head_sums(x32 * q, heads_of[...])
    dv = head_sums(x32 * bd, heads_of[...])
    dw = dv * w_end * dt
    carried = head_sums(jnp.broadcast_to(gain_sum, (SUB, inner)), heads_of[...])[0:1]
    constant = jnp.sum(dw, 0, keepdims=True) + carried
    up = tri_up.astype(f32).astype(bf16)
    inward = jnp.where(real, flow_sum - dw, 0.0)
    dstep = fold_lanes(dot(up, split_pack(inward, heads)), heads) + constant
    dstep = jnp.where(real, dstep, 0.0)
    ddt = ddt + dstep * head_par[1:2]
    dpre = jnp.where(real, ddt * sigmoid(v), 0.0)
    head_out[0:1] += jnp.sum(dstep * dt, 0, keepdims=True)
    head_out[1:2] += jnp.sum(dpre, 0, keepdims=True)
    dcat[:, mixed + inner:] = dpre.astype(bf16)

    masks = [None] + [jnp.broadcast_to(tok[:, k:k + 1], (GROUP, LANE)) for k in (1, 2, 3)]
    for start in range(0, mixed, LANE):
        cols = slice(start, start + LANE)
        if start < inner:
            dact = dt_wide[:, cols] * q[:, cols] + chan[0:1, cols] * dy32[:, cols]
        elif start < inner + state_dim:
            dact = db[:, start - inner:start - inner + LANE]
        else:
            dact = dc[:, start - inner - state_dim:start - inner - state_dim + LANE]
        dconv = dact * slopes[start // LANE]
        pre = xb_pre[:, cols]
        conv_out[4:5, cols] += jnp.sum(dconv, 0, keepdims=True)
        conv_out[3:4, cols] += jnp.sum(dconv * pre, 0, keepdims=True)
        dpre_cols = taps[3:4, cols] * dconv
        for k, ext in ((1, ext1), (2, ext2), (3, ext3)):
            ext[0:GROUP, cols] = dconv * masks[k]
            shifted = ext[k:k + GROUP, cols]
            dpre_cols = dpre_cols + taps[3 - k:4 - k, cols] * shifted
            conv_out[3 - k:4 - k, cols] += jnp.sum(shifted * pre, 0, keepdims=True)
        dcat[:, cols] = dpre_cols.astype(bf16)

    grads = dcat[...]
    per = dh0.shape[1] // LANE
    norm_dot = jnp.zeros((GROUP, LANE), f32)
    for rel, dh in enumerate((dh0, dh1, dh2, dh3)):
        absolute = jnp.bitwise_xor(me, rel)
        places = [meta[1 + absolute * per + half] for half in range(per)]
        weight = jnp.concatenate([w[block_slice(place), :] for place in places], 0)
        part = dot(grads, weight, 1, 1)
        dh[...] = part.astype(bf16)
        for half, place in enumerate(places):
            cols = slice(half * LANE, (half + 1) * LANE)
            norm_dot = norm_dot + part[:, cols] * hid[:, block_slice(place)].astype(f32)
    nd_out[0] = to_rows(jnp.sum(norm_dot, -1, keepdims=True))


def last_kernel(
    width, rows, cot, dh, got, nd0, nd1, nd2, nd3, rs_row, gain, grad, gain_out
):
    step = pl.program_id(0)

    @pl.when(step == 0)
    def _():
        gain_out[...] = jnp.zeros(gain_out.shape, f32)

    rs = to_column(rs_row[0])
    mean = to_column(nd0[0] + nd1[0] + nd2[0] + nd3[0]) / width
    normed = rows[...].astype(f32) * rs
    total = dh[...].astype(f32) + got[...].astype(f32)
    gain_out[0:1] += jnp.sum(total * normed, 0, keepdims=True)
    grad[...] = (cot[...].astype(f32) + rs * (total * gain[...] - normed * mean)).astype(bf16)


def smem():
    return pl.BlockSpec(memory_space=pltpu.SMEM)


def whole(array):
    zeros = (0,) * array.ndim
    return pl.BlockSpec(array.shape, lambda i: zeros)


def run(kernel, steps, ins, outs, scratch, flops, bytes_accessed):
    return pl.pallas_call(
        kernel,
        grid=(steps,),
        in_specs=[spec for _, spec in ins],
        out_specs=[spec for _, spec in outs],
        out_shape=[shape for shape, _ in outs],
        scratch_shapes=scratch,
        compiler_params=pltpu.CompilerParams(
            vmem_limit_bytes=VMEM_LIMIT, dimension_semantics=("arbitrary",)
        ),
        cost_estimate=pl.CostEstimate(
            flops=flops, bytes_accessed=bytes_accessed, transcendentals=0
        ),
    )(*[array for array, _ in ins])


def ring_order(count):
    return list(range(0, count, 2)) + list(range(count - 1 - count % 2, 0, -2))


def ring_pairs(count, shift):
    order = ring_order(count)
    return [(order[i], order[(i + shift) % count]) for i in range(count)]


def head_swap(array, rel):
    count = lax.axis_size("head")
    return lax.ppermute(array, "head", [(i, i ^ rel) for i in range(count)])


def ring_gather(block):
    count = lax.axis_size("fsdp")
    blocks = [None] * count
    blocks[0] = ahead = back = block
    for step in range(1, count // 2 + 1):
        ahead = lax.ppermute(ahead, "fsdp", ring_pairs(count, 1))
        blocks[step] = ahead
        if step < count - step:
            back = lax.ppermute(back, "fsdp", ring_pairs(count, -1))
            blocks[count - step] = back
    return blocks


def ring_scatter(blocks):
    count = lax.axis_size("fsdp")
    got = [lax.ppermute(blocks[i], "fsdp", ring_pairs(count, -i)) for i in range(1, count)]
    total = blocks[0].astype(f32)
    for part in got:
        total = total + part.astype(f32)
    return total


def head_gather(own):
    far = head_swap(own, 2)
    return [own, head_swap(own, 1), far, head_swap(far, 1)]


def shards(
    block_in, segment_ids, norm_gain, proj_z, proj_x, proj_bc, proj_dt, conv_x, bias_x, conv_bc,
    bias_bc, dt_bias, a_log, skip_d, gate_gain, proj_out, cotangent,
):
    seqs, seq_len = segment_ids.shape
    tokens = seqs * seq_len
    head_devs = lax.axis_size("head")
    fsdp_devs = lax.axis_size("fsdp")
    me = lax.axis_index("head")
    width_part = block_in.shape[1]
    width = width_part * head_devs
    heads = dt_bias.shape[0]
    inner = bias_x.shape[0]
    head_dim = inner // heads
    inner_full = inner * head_devs
    state_dim = conv_bc.shape[1] // 2
    mixed = inner + 2 * state_dim
    n_groups = seq_len // GROUP
    feature_blocks = width // LANE
    ringed = fsdp_devs == feature_blocks
    cat = mixed + inner + LANE

    w_mine = jnp.concatenate(
        [proj_x, proj_bc, proj_z, jnp.pad(proj_dt, ((0, 0), (0, LANE - heads)))], 1
    )
    if ringed:
        order = ring_order(fsdp_devs)
        position = jnp.array([order.index(i) for i in range(fsdp_devs)], jnp.int32)
        mine = position[lax.axis_index("fsdp")]
        places = jnp.mod(mine - position, fsdp_devs)
        w = jnp.concatenate(ring_gather(w_mine), 0)
        w_out = jnp.stack(ring_gather(proj_out), 0)
    else:
        places = jnp.arange(feature_blocks, dtype=jnp.int32)
        w = lax.all_gather(w_mine, "fsdp", axis=0, tiled=True)
        w_out = lax.all_gather(proj_out, "fsdp", axis=1, tiled=True)
        w_out = w_out.reshape(inner, feature_blocks, LANE).transpose(1, 0, 2)
    meta = jnp.concatenate([me[None].astype(jnp.int32), places])

    seg = segment_ids
    before = [jnp.pad(seg, ((0, 0), (k, 0)), constant_values=-1)[:, :seq_len] for k in (1, 2, 3)]
    seg_groups = seg.reshape(seqs, n_groups, GROUP)
    end_seg = seg_groups[:, :, -1]
    prev_seg = jnp.pad(end_seg, ((0, 0), (1, 0)), constant_values=-1)[:, :n_groups]
    link = (end_seg == prev_seg).astype(f32)
    tok = jnp.stack(
        [seg.astype(f32)]
        + [(b == seg).astype(f32) for b in before]
        + [
            (seg_groups == end_seg[:, :, None]).astype(f32).reshape(seqs, seq_len),
            (seg_groups == prev_seg[:, :, None]).astype(f32).reshape(seqs, seq_len),
        ]
        + [jnp.zeros(seg.shape, f32)] * 2,
        -1,
    ).reshape(tokens, 8)
    seg_row = seg.astype(f32).reshape(seqs * n_groups, 1, GROUP)

    rate = -jnp.exp(a_log)
    taps = jnp.pad(
        jnp.concatenate(
            [
                jnp.concatenate([conv_x, conv_bc], 1),
                jnp.concatenate([bias_x, bias_bc])[None],
            ],
            0,
        ),
        ((0, 3), (0, 0)),
    )
    head_par = jnp.pad(jnp.stack([dt_bias, rate]), ((0, 6), (0, LANE - heads)))
    chan = jnp.pad(jnp.stack([jnp.repeat(skip_d, head_dim), gate_gain]), ((0, 6), (0, 0)))
    lanes = jnp.arange(LANE)[:, None]
    owners = (jnp.arange(inner) // head_dim)[None]
    spread = ((lanes % heads == owners) & (lanes < 3 * heads)).astype(bf16)
    heads_of = (lanes == owners).astype(bf16).T
    gain = norm_gain[None]
    gain_mine = lax.dynamic_slice_in_dim(gain, me * width_part, width_part, 1)

    token_shape = lambda cols, dtype: jax.ShapeDtypeStruct((seq_len, cols), dtype)
    row_shape = jax.ShapeDtypeStruct((n_groups, SUB, GROUP), f32)
    seq_rows = [slice(s * seq_len, (s + 1) * seq_len) for s in range(seqs)]

    def part(cols, base=0, back=False):
        if back:
            return pl.BlockSpec((GROUP, cols), lambda i: (base + n_groups - 1 - i, 0))
        return pl.BlockSpec((GROUP, cols), lambda i: (base + i, 0))

    def row_part(rows=SUB, base=0, back=False):
        if back:
            return pl.BlockSpec((1, rows, GROUP), lambda i: (base + n_groups - 1 - i, 0, 0))
        return pl.BlockSpec((1, rows, GROUP), lambda i: (base + i, 0, 0))

    def forward(s, rows):
        base = s * n_groups
        ins = [(meta, smem()), (link[s], smem())]
        ins += [(r, part(width_part)) for r in rows]
        ins += [(tok, part(8, base)), (seg_row, row_part(1, base))]
        ins += [(a, whole(a)) for a in (w, gain, taps, head_par, chan, spread)]
        outs = [
            (token_shape(width, bf16), part(width)),
            (token_shape(mixed, f32), part(mixed)),
            (token_shape(mixed, f32), part(mixed)),
            (token_shape(inner, f32), part(inner)),
            (token_shape(LANE, f32), part(LANE)),
            (token_shape(LANE, f32), part(LANE)),
            (token_shape(inner, f32), part(inner)),
            (
                jax.ShapeDtypeStruct((n_groups, state_dim, inner), f32),
                pl.BlockSpec((1, state_dim, inner), lambda i: (i, 0, 0)),
            ),
            (row_shape, row_part()),
            (row_shape, row_part()),
        ]
        scratch = [pltpu.VMEM((GROUP + SUB, mixed), f32), pltpu.VMEM((state_dim, inner), f32)]
        kernel = functools.partial(forward_kernel, heads, head_dim, state_dim)
        return run(kernel, n_groups, ins, outs, scratch, 12 * 10**9, 20 * 2**20)

    def gate(s, squares, z, y, cots):
        ins = [(meta, smem())] + [(a, row_part()) for a in squares]
        ins += [(z, part(inner)), (y, part(inner))]
        ins += [(c, part(width_part)) for c in cots]
        ins += [(w_out, whole(w_out)), (chan, whole(chan))]
        gain_shape = jax.ShapeDtypeStruct((SUB, inner), f32)
        outs = [(token_shape(width_part, bf16), part(width_part))] * 4 + [
            (token_shape(inner, bf16), part(inner)),
            (token_shape(inner, f32), part(inner)),
            (token_shape(width, bf16), part(width)),
            (row_shape, row_part()),
            (gain_shape, whole(gain_shape)),
        ]
        kernel = functools.partial(gate_kernel, inner_full)
        return run(kernel, n_groups, ins, outs, [], 6 * 10**9, 12 * 2**20)

    def backward(s, squares, dots, z, y, dyn, xb_pre, xb_conv, v, cum, enter, hid):
        base = s * n_groups
        ins = [(meta, smem()), (link[s], smem())]
        ins += [(a, row_part(back=True)) for a in (*squares, *dots)]
        ins += [(a, part(a.shape[1], back=True)) for a in (z, y, dyn, xb_pre, xb_conv, v, cum)]
        ins += [(
            enter,
            pl.BlockSpec((1, state_dim, inner), lambda i: (n_groups - 1 - i, 0, 0)),
        )]
        ins += [(tok, part(8, base, True)), (seg_row, row_part(1, base, True))]
        ins += [(hid, part(width, back=True))]
        ins += [(a, whole(a)) for a in (w, taps, head_par, chan, spread, heads_of)]
        conv_shape = jax.ShapeDtypeStruct((SUB, mixed), f32)
        head_shape = jax.ShapeDtypeStruct((SUB, LANE), f32)
        skip_shape = jax.ShapeDtypeStruct((SUB, inner), f32)
        outs = [(token_shape(cat, bf16), part(cat, back=True))]
        outs += [(token_shape(width_part, bf16), part(width_part, back=True))] * 4
        outs += [(row_shape, row_part(back=True))]
        outs += [(a, whole(a)) for a in (conv_shape, head_shape, skip_shape)]
        scratch = [pltpu.VMEM((GROUP + SUB, mixed), f32)] * 3
        scratch += [pltpu.VMEM((state_dim, inner), f32)]
        kernel = functools.partial(
            backward_kernel, heads, head_dim, state_dim, inner_full, n_groups
        )
        return run(kernel, n_groups, ins, outs, scratch, 30 * 10**9, 25 * 2**20)

    def last(s, dh, got, dots, rs_row):
        base = s * n_groups
        gain_shape = jax.ShapeDtypeStruct((SUB, width_part), f32)
        ins = [(block_in, part(width_part, base)), (cotangent, part(width_part, base))]
        ins += [(dh, part(width_part)), (got, part(width_part))]
        ins += [(a, row_part()) for a in dots] + [(rs_row, row_part())]
        ins += [(gain_mine, whole(gain_mine))]
        outs = [(token_shape(width_part, bf16), part(width_part)), (gain_shape, whole(gain_shape))]
        return run(
            functools.partial(last_kernel, width), n_groups, ins, outs, [], 10**6, 4 * 2**20
        )

    def scatter_far(parts):
        near = parts[0].astype(f32) + head_swap(parts[1], 1).astype(f32)
        far = (parts[2].astype(f32) + head_swap(parts[3], 1).astype(f32)).astype(bf16)
        return near, head_swap(far, 2)

    def spread_rows(rows):
        return [rows] + [head_swap(rows, rel) for rel in (1, 2, 3)]

    row_parts = [head_gather(block_in[rows]) for rows in seq_rows]
    cot_parts = [head_gather(cotangent[rows]) for rows in seq_rows]

    fwd = [forward(s, row_parts[s]) for s in range(seqs)]
    squares = [spread_rows(f[8]) for f in fwd]
    gates = [gate(s, squares[s], fwd[s][3], fwd[s][6], cot_parts[s]) for s in range(seqs)]
    dots = [spread_rows(g[7]) for g in gates]
    out_rows = []
    for s in range(seqs):
        near, far = scatter_far(gates[s][:4])
        out_rows.append((block_in[seq_rows[s]].astype(f32) + near + far.astype(f32)).astype(bf16))
    yn = jnp.concatenate([g[4] for g in gates], 0)
    cot_whole = jnp.concatenate([g[6] for g in gates], 0)
    g_out = dot(cot_whole, yn, 0, 0).astype(bf16)

    bwd = []
    for s in range(seqs):
        hid, xb_pre, xb_conv, z, v, cum, y, enter = fwd[s][:8]
        bwd.append(
            backward(
                s, squares[s], dots[s], z, y, gates[s][5], xb_pre, xb_conv, v, cum, enter, hid
            )
        )
    hidden = jnp.concatenate([f[0] for f in fwd], 0)
    dcat = jnp.concatenate([b[0] for b in bwd], 0)
    g_cat = dot(hidden, dcat, 0, 0)
    g_x = g_cat[:, :inner].astype(bf16)
    g_bc = g_cat[:, inner:mixed].astype(bf16)
    g_z = g_cat[:, mixed:mixed + inner].astype(bf16)
    g_dt = g_cat[:, mixed + inner:].astype(bf16)

    bc_part = 2 * state_dim // head_devs
    g_bc = g_bc.reshape(width, head_devs, bc_part).transpose(1, 0, 2)
    bc_rel = [lax.dynamic_index_in_dim(g_bc, me ^ rel, 0, False) for rel in range(4)]
    g_bc_mine = bc_rel[0].astype(f32)
    for rel in (1, 2, 3):
        g_bc_mine = g_bc_mine + head_swap(bc_rel[rel], rel).astype(f32)
    g_side = jnp.concatenate(
        [jnp.pad(g_bc_mine.astype(bf16), ((0, 0), (0, LANE - bc_part))), g_dt], 1
    )

    if ringed:
        blocks = lambda a: [a[i * LANE:(i + 1) * LANE] for i in range(fsdp_devs)]
        s_x = ring_scatter(blocks(g_x))
        s_z = ring_scatter(blocks(g_z))
        s_side = ring_scatter(blocks(g_side))
        s_out = ring_scatter(blocks(g_out)).T
    else:
        scatter = lambda a: lax.psum_scatter(
            a.astype(f32), "fsdp", scatter_dimension=0, tiled=True
        )
        s_x, s_z, s_side = scatter(g_x), scatter(g_z), scatter(g_side)
        s_out = scatter(g_out).T
    s_bc, s_dt = s_side[:, :bc_part], s_side[:, LANE:LANE + heads]

    grad_rows, gain_sums = [], []
    for s in range(seqs):
        near, far = scatter_far(bwd[s][1:5])
        rows, gain_sum = last(s, near, far, spread_rows(bwd[s][5]), fwd[s][9])
        grad_rows.append(rows)
        gain_sums.append(gain_sum)

    g_conv = sum([b[6] for b in bwd])
    g_head = sum([b[7] for b in bwd])
    g_skip = sum([b[8] for b in bwd])[0].reshape(heads, head_dim).sum(1)
    g_gate = sum([g[8] for g in gates])[0]
    small = lax.psum(
        (
            sum(gain_sums)[0],
            g_conv[:, :inner],
            g_gate,
            jnp.concatenate([g_head[0, :heads] * rate, g_head[1, :heads], g_skip]),
        ),
        "fsdp",
    )
    bc_small = lax.psum(g_conv[:, inner:], ("fsdp", "head"))
    n_gain, conv_sums, gate_sums, head_part = small
    return (
        jnp.concatenate(out_rows, 0),
        jnp.concatenate(grad_rows, 0),
        n_gain,
        s_z,
        s_x,
        s_bc,
        s_dt,
        conv_sums[:4],
        conv_sums[4],
        bc_small[:4],
        bc_small[4],
        head_part[heads:2 * heads],
        head_part[:heads],
        head_part[2 * heads:],
        gate_sums,
        s_out,
    )


def solution(mesh):
    in_specs = (
        P("fsdp", "head"), P("fsdp", None), P(), P("fsdp", "head"), P("fsdp", "head"),
        P("fsdp", None), P("fsdp", "head"), P(None, "head"), P("head"), P(), P(), P("head"),
        P("head"), P("head"), P("head"), P("head", "fsdp"), P("fsdp", "head"),
    )
    out_specs = (
        P("fsdp", "head"), P("fsdp", "head"), P("head"), P("fsdp", "head"), P("fsdp", "head"),
        P("fsdp", "head"), P("fsdp", "head"), P(None, "head"), P("head"), P(), P(), P("head"),
        P("head"), P("head"), P("head"), P("head", "fsdp"),
    )
    return jax.shard_map(shards, mesh=mesh, in_specs=in_specs, out_specs=out_specs, check_vma=False)
```

```python
import functools

import jax
import jax.numpy as jnp
import numpy as np
from jax import lax
from jax.experimental import pallas as pl
from jax.experimental.pallas import tpu as pltpu
from jax.sharding import PartitionSpec as P

GROUP = 256
LANE = 128
SUB = 8

epsilon = 1e-05
neg_big = -1e30
f32 = jnp.float32
bf16 = jnp.bfloat16

VMEM_LIMIT = 56 * 1024 * 1024


def dot(left, right, left_dim=1, right_dim=0):
    return lax.dot_general(
        left, right, (((left_dim,), (right_dim,)), ((), ())), preferred_element_type=f32
    )


def sigmoid(values):
    return 1.0 / (1.0 + jnp.exp(-values))


def softplus(values):
    return jnp.maximum(values, 0.0) + jnp.log1p(jnp.exp(-jnp.abs(values)))


def split_pack(values, count):
    high = values.astype(bf16).astype(f32)
    rest = values - high
    mid = rest.astype(bf16).astype(f32)
    last = rest - mid
    packed = high + pltpu.roll(mid, count, 1) + pltpu.roll(last, 2 * count, 1)
    return packed.astype(bf16)


def fold_lanes(values, count):
    lanes = values.shape[1]
    return values + pltpu.roll(values, lanes - count, 1) + pltpu.roll(values, lanes - 2 * count, 1)


def triangle(size, upper):
    row = lax.broadcasted_iota(jnp.int32, (size, size), 0)
    col = lax.broadcasted_iota(jnp.int32, (size, size), 1)
    return (row <= col if upper else row >= col)


def head_sums(values, heads_of):
    high = values.astype(bf16)
    low = (values - high.astype(f32)).astype(bf16)
    return dot(high, heads_of) + dot(low, heads_of)


def to_rows(column):
    wide = jnp.broadcast_to(column, (column.shape[0], LANE))
    return wide.T[:SUB]


def to_column(rows):
    return rows.T[:, :1]


def column_of(refs):
    return jnp.concatenate(
        [to_column(sum([ref[i] for ref in refs])) for i in range(refs[0].shape[0])], 0
    )


def rows_of(column, ref):
    for i in range(ref.shape[0]):
        ref[i] = to_rows(column[i * GROUP:(i + 1) * GROUP])


def block_slice(index):
    return pl.ds(pl.multiple_of(index * LANE, LANE), LANE)


def segment_rows(seg, seq, group):
    start = pl.multiple_of(jnp.maximum(group * GROUP - LANE, 0), LANE)
    now = seg[seq:seq + 1, pl.ds(pl.multiple_of(group * GROUP, GROUP), GROUP)].astype(f32)
    old = jnp.where(group > 0, seg[seq:seq + 1, pl.ds(start, LANE)].astype(f32), -1.0)
    both = jnp.broadcast_to(jnp.concatenate([old, now], 1), (SUB, LANE + GROUP))
    end, prev = now[:, GROUP - 1:], old[:, LANE - 1:]
    now_rows = jnp.broadcast_to(now, (SUB, GROUP))
    row = lax.broadcasted_iota(jnp.int32, (SUB, GROUP), 0)
    rows = jnp.where(row == 0, now_rows, 0.0)
    for k in (1, 2, 3):
        same = pltpu.roll(both, k, 1)[:, LANE:] == now_rows
        rows = jnp.where((row == k) & same, 1.0, rows)
    rows = jnp.where((row == 4) & (now_rows == end), 1.0, rows)
    rows = jnp.where((row == 5) & (now_rows == prev), 1.0, rows)
    return now, rows.T, (end == prev).astype(f32)


def scan_terms(cum, dt, tok, link, head_par, spread, heads):
    lane = lax.broadcasted_iota(jnp.int32, (GROUP, LANE), 1)
    real = lane < heads
    end = cum[GROUP - 1:GROUP]
    ain = jnp.where(real, jnp.exp(cum) * tok[:, 5:6], 0.0)
    w_end = jnp.where(real, jnp.exp(end - cum) * tok[:, 4:5], 0.0)
    carry = jnp.where(real[:SUB], jnp.exp(jnp.broadcast_to(end, (SUB, LANE))) * link, 0.0)
    wide = dot(
        jnp.concatenate([split_pack(a, heads) for a in (dt, ain, w_end, carry, head_par)], 0),
        spread,
    )
    cuts = [wide[i * GROUP:(i + 1) * GROUP] for i in range(3)]
    carry_wide = wide[3 * GROUP:3 * GROUP + 1]
    skip = wide[3 * GROUP + SUB + 2:3 * GROUP + SUB + 3]
    return w_end, cuts, carry_wide, skip


def join_kernel(lanes, z, out, x, bc, dt, late, early):
    inner, mixed = z.shape[1], x.shape[1] + bc.shape[1]
    late[:, :inner] = z[...]
    late[:, inner:] = out[...].T
    early[:, :inner] = x[...]
    early[:, inner:mixed] = bc[...]
    early[:, mixed:] = jnp.concatenate(
        [dt[...], jnp.zeros((lanes - dt.shape[0], dt.shape[1]), bf16)], 0
    ).T


def forward_kernel(
    heads, head_dim, state_dim, seq,
    meta, row0, row1, row2, row3, seg, w_x, w_z, gain, conv_x, conv_bc, bias_x, bias_bc, head_par, spread,
    hid, xb_pre, xb_conv, z_out, v_out, cum_out, y_out, enter_out, rs_out, sq_out,
    ext, held,
):
    inner = heads * head_dim
    mixed = inner + 2 * state_dim
    step = pl.program_id(0)
    me = meta[0]
    parts = [ref[...].astype(f32) for ref in (row0, row1, row2, row3)]
    total = sum([jnp.sum(part * part, -1, keepdims=True) for part in parts])
    width = 4 * parts[0].shape[1]
    rs = lax.rsqrt(total / width + epsilon)
    rs_out[0] = to_rows(rs)
    per = parts[0].shape[1] // LANE
    for rel in range(4):
        absolute = jnp.bitwise_xor(me, rel)
        for half in range(per):
            feature = absolute * per + half
            scale = gain[:, block_slice(feature)]
            part = parts[rel][:, half * LANE:(half + 1) * LANE]
            hid[:, block_slice(meta[1 + feature])] = (part * rs * scale).astype(bf16)
    hidden = hid[...]

    @pl.when(step == 0)
    def _():
        ext[0:SUB] = jnp.zeros((SUB, mixed), f32)
        held[...] = jnp.zeros(held.shape, f32)

    @pl.when(step > 0)
    def _():
        ext[0:SUB] = ext[GROUP:GROUP + SUB]

    seg_row, tok, link = segment_rows(seg, seq, step)
    pre = dot(hidden, w_x[:, :mixed])
    ext[SUB:SUB + GROUP] = pre
    xb_pre[...] = pre
    z = dot(hidden, w_z[...])
    z_out[...] = z
    masks = [None] + [jnp.broadcast_to(tok[:, k:k + 1], (GROUP, LANE)) for k in (1, 2, 3)]
    acts = []
    for start in range(0, mixed, LANE):
        cols = slice(start, start + LANE)
        taps, bias = (conv_x, bias_x) if start < inner else (conv_bc, bias_bc)
        own = cols if start < inner else slice(start - inner, start - inner + LANE)
        conv = bias[:, own] + taps[3:4, own] * ext[SUB:SUB + GROUP, cols]
        for k in (1, 2, 3):
            conv = conv + taps[3 - k:4 - k, own] * (ext[SUB - k:SUB - k + GROUP, cols] * masks[k])
        xb_conv[:, cols] = conv
        acts.append((conv * sigmoid(conv)).astype(bf16))
    x = jnp.concatenate(acts[:inner // LANE], 1)
    b = jnp.concatenate(acts[inner // LANE:(inner + state_dim) // LANE], 1)
    c = jnp.concatenate(acts[(inner + state_dim) // LANE:], 1)

    lane = lax.broadcasted_iota(jnp.int32, (GROUP, LANE), 1)
    real = lane < heads
    v = dot(hidden, w_x[:, mixed:]) + head_par[0:1]
    v_out[...] = v
    dt = jnp.where(real, softplus(v), 0.0)
    tri = triangle(GROUP, False)
    tri_low = tri.astype(f32).astype(bf16)
    cum = fold_lanes(dot(tri_low, split_pack(dt * head_par[1:2], heads)), heads)
    cum = jnp.where(real, cum, 0.0)
    cum_out[...] = cum
    cum_t = cum.T
    _, (dt_wide, ain_wide, end_wide), carry_wide, skip = scan_terms(
        cum, dt, tok, link, head_par[...], spread[...], heads
    )
    x32 = x.astype(f32)
    xdt32 = x32 * dt_wide
    xdt = xdt32.astype(bf16)
    xw = (xdt32 * end_wide).astype(bf16)

    gram = dot(c, b, 1, 1)
    allowed = tri & (tok[:, 0:1] == seg_row)
    off = jnp.where(allowed, 0.0, neg_big)
    first = lane < head_dim
    entering = held[...]
    enter_out[0] = entering
    u = dot(c, entering.astype(bf16))
    gated_sq = jnp.zeros((GROUP, LANE), f32)
    zero = jnp.zeros((GROUP, LANE), bf16)
    for pair in range(heads // 2):
        cols = slice(pair * LANE, (pair + 1) * LANE)
        xp = xdt[:, cols]
        intra = 0.0
        for odd in range(2):
            head = 2 * pair + odd
            decay = jnp.exp(cum[:, head:head + 1] - cum_t[head:head + 1] + off)
            weight = (gram * decay).astype(bf16)
            mine = jnp.where(first, xp, zero) if odd == 0 else jnp.where(first, zero, xp)
            intra = intra + dot(weight, mine)
        y = intra + ain_wide[:, cols] * u[:, cols] + skip[:, cols] * x32[:, cols]
        y_out[:, cols] = y
        zc = z[:, cols]
        gated = y * zc * sigmoid(zc)
        gated_sq = gated_sq + gated * gated
    held[...] = dot(b, xw, 0, 0) + carry_wide * entering
    sq_out[0] = to_rows(jnp.sum(gated_sq, -1, keepdims=True))


def gate_kernel(
    inner_full,
    meta, sq0, sq1, sq2, sq3, z, y, cot0, cot1, cot2, cot3, w_out, gate_gain, gain_in,
    out0, out1, out2, out3, yn_out, dyn_out, cot_out, gd_out, rs_out, gain_out,
):
    step = pl.program_id(0)
    me = meta[0]
    square = column_of([sq0, sq1, sq2, sq3])
    rs = lax.rsqrt(square / inner_full + epsilon)
    rows_of(rs, rs_out)
    inner = z.shape[1]
    strips = [slice(s, s + LANE) for s in range(0, inner, LANE)]
    norms, gates = [], []
    for cols in strips:
        zc = z[:, cols]
        gated = y[:, cols] * zc * sigmoid(zc)
        gnorm = gated * rs
        gates.append(gated)
        norms.append(gnorm)
        yn_out[:, cols] = (gnorm * gate_gain[:, cols]).astype(bf16)
    yn = yn_out[...]
    per = cot0.shape[1] // LANE
    dyn = 0.0
    for rel, (cot, out) in enumerate(((cot0, out0), (cot1, out1), (cot2, out2), (cot3, out3))):
        absolute = jnp.bitwise_xor(me, rel)
        places = [meta[1 + absolute * per + half] for half in range(per)]
        weight = jnp.concatenate([w_out[block_slice(place), :] for place in places], 0)
        out[...] = dot(yn, weight, 1, 1).astype(bf16)
        cv = cot[...]
        dyn = dyn + dot(cv, weight)
        for half, place in enumerate(places):
            cot_out[:, block_slice(place)] = cv[:, half * LANE:(half + 1) * LANE]
    dyn_out[...] = dyn

    @pl.when(step == 0)
    def _():
        gain_out[...] = gain_in[...]

    gd = jnp.zeros((z.shape[0], LANE), f32)
    for index, cols in enumerate(strips):
        dc = dyn[:, cols]
        gd = gd + dc * gate_gain[:, cols] * gates[index]
        gain_out[0:1, cols] += jnp.sum(dc * norms[index], 0, keepdims=True)
    rows_of(jnp.sum(gd, -1, keepdims=True), gd_out)


def gate_back_kernel(inner_full, rs_row, gd0, gd1, gd2, gd3, z, y, dyn, gate_gain, dy_out, dz_out):
    rs = column_of([rs_row])
    inner_dot = column_of([gd0, gd1, gd2, gd3]) * rs / inner_full
    for start in range(0, z.shape[1], LANE):
        cols = slice(start, start + LANE)
        zc, yc = z[:, cols], y[:, cols]
        sg = sigmoid(zc)
        zs = zc * sg
        gnorm = yc * zs * rs
        dgated = rs * (dyn[:, cols] * gate_gain[:, cols] - gnorm * inner_dot)
        dy_out[:, cols] = (dgated * zs).astype(bf16)
        dz_out[:, cols] = (dgated * yc * (sg * (1.0 + zc * (1.0 - sg)))).astype(bf16)


def backward_kernel(
    heads, head_dim, state_dim, last_group, seq, fresh,
    meta, dy_in, dz_in, y, xb_pre, xb_conv, v_in, cum_in, enter_in, hid,
    seg, w_x, w_z, conv_x, conv_bc, head_par, spread, heads_of, sums_in, dheld_in, edge_in,
    dcat, dh0, nd_out, dh1, dh2, dh3, sums, dheld, edge,
    ext1, ext2, ext3,
):
    inner = heads * head_dim
    mixed = inner + 2 * state_dim
    step = pl.program_id(0)
    group = last_group - step
    me = meta[0]

    @pl.when(step == 0)
    def _():
        dheld[...] = jnp.zeros(dheld.shape, f32) if fresh else dheld_in[...]
        edge[...] = jnp.zeros(edge.shape, f32) if fresh else edge_in[...]
        sums[...] = sums_in[...]

    for k, ext in enumerate((ext1, ext2, ext3)):
        ext[GROUP:GROUP + SUB] = edge[k * SUB:(k + 1) * SUB]

    seg_row, tok, link = segment_rows(seg, seq, group)
    dy = dy_in[...]
    dy32 = dy.astype(f32)
    acts, slopes = [], []
    for start in range(0, mixed, LANE):
        conv = xb_conv[:, start:start + LANE]
        sg = sigmoid(conv)
        acts.append((conv * sg).astype(bf16))
        slopes.append(sg * (1.0 + conv * (1.0 - sg)))
    x = jnp.concatenate(acts[:inner // LANE], 1)
    b = jnp.concatenate(acts[inner // LANE:(inner + state_dim) // LANE], 1)
    c = jnp.concatenate(acts[(inner + state_dim) // LANE:], 1)
    x32 = x.astype(f32)

    lane = lax.broadcasted_iota(jnp.int32, (GROUP, LANE), 1)
    real = lane < heads
    v = v_in[...]
    dt = jnp.where(real, softplus(v), 0.0)
    cum = cum_in[...]
    cum_t = cum.T
    w_end, (dt_wide, ain_wide, end_wide), carry_wide, skip = scan_terms(
        cum, dt, tok, link, head_par[...], spread[...], heads
    )
    xdt32 = x32 * dt_wide
    xdt = xdt32.astype(bf16)
    xw = (xdt32 * end_wide).astype(bf16)

    entering = enter_in[0]
    enter_low = entering.astype(bf16)
    dstate = dheld[...]
    dstate_low = dstate.astype(bf16)
    dyw = (dy32 * ain_wide).astype(bf16)
    dc = dot(dyw, enter_low, 1, 1)
    db = dot(xw, dstate_low, 1, 1)
    bd = dot(b, dstate_low)
    gain_sum = jnp.sum(dstate * entering, 0, keepdims=True) * carry_wide
    dheld[...] = dot(c, dyw, 0, 0) + carry_wide * dstate

    gram_t = dot(b, c, 1, 1)
    tri_up = triangle(GROUP, True)
    off = jnp.where(tri_up & (tok[:, 0:1] == seg_row), 0.0, neg_big)
    first = lane < head_dim
    zero = jnp.zeros((GROUP, LANE), bf16)
    dgram_t = jnp.zeros((GROUP, GROUP), f32)
    flow, through = [], []
    for pair in range(heads // 2):
        cols = slice(pair * LANE, (pair + 1) * LANE)
        xp, dyp = xdt[:, cols], dy[:, cols]
        dxw = 0.0
        for odd in range(2):
            head = 2 * pair + odd
            decay = jnp.exp(cum_t[head:head + 1] - cum[:, head:head + 1] + off)
            weight = (gram_t * decay).astype(bf16)
            own_dy = jnp.where(first, dyp, zero) if odd == 0 else jnp.where(first, zero, dyp)
            own_x = jnp.where(first, xp, zero) if odd == 0 else jnp.where(first, zero, xp)
            dxw = dxw + dot(weight, own_dy)
            dgram_t = dgram_t + dot(own_x, dyp, 1, 1) * decay
        x_cols, dy_cols = x32[:, cols], dy32[:, cols]
        ymix = y[:, cols] - skip[:, cols] * x_cols
        flow.append(dy_cols * ymix - xp.astype(f32) * dxw)
        through.append(dxw + end_wide[:, cols] * bd[:, cols])
        sums[0:1, mixed + pair * LANE:mixed + (pair + 1) * LANE] += jnp.sum(
            dy_cols * x_cols, 0, keepdims=True
        )
    dgram_low = dgram_t.astype(bf16)
    db = db + dot(dgram_low, c)
    dc = dc + dot(dgram_low, b, 0, 0)
    q = jnp.concatenate(through, 1)
    flow_sum = head_sums(jnp.concatenate(flow, 1), heads_of[...])
    ddt = head_sums(x32 * q, heads_of[...])
    dv = head_sums(x32 * bd, heads_of[...])
    dw = dv * w_end * dt
    carried = head_sums(jnp.broadcast_to(gain_sum, (SUB, inner)), heads_of[...])[0:1]
    constant = jnp.sum(dw, 0, keepdims=True) + carried
    up = tri_up.astype(f32).astype(bf16)
    inward = jnp.where(real, flow_sum - dw, 0.0)
    dstep = fold_lanes(dot(up, split_pack(inward, heads)), heads) + constant
    dstep = jnp.where(real, dstep, 0.0)
    ddt = ddt + dstep * head_par[1:2]
    dpre = jnp.where(real, ddt * sigmoid(v), 0.0)
    sums[2:3, mixed:mixed + LANE] += jnp.sum(dstep * dt, 0, keepdims=True)
    sums[3:4, mixed:mixed + LANE] += jnp.sum(dpre, 0, keepdims=True)
    dcat[:, mixed:] = dpre.astype(bf16)

    masks = [None] + [jnp.broadcast_to(tok[:, k:k + 1], (GROUP, LANE)) for k in (1, 2, 3)]
    for start in range(0, mixed, LANE):
        cols = slice(start, start + LANE)
        taps = conv_x if start < inner else conv_bc
        own = cols if start < inner else slice(start - inner, start - inner + LANE)
        if start < inner:
            dact = dt_wide[:, cols] * q[:, cols] + skip[:, cols] * dy32[:, cols]
        elif start < inner + state_dim:
            dact = db[:, start - inner:start - inner + LANE]
        else:
            dact = dc[:, start - inner - state_dim:start - inner - state_dim + LANE]
        dconv = dact * slopes[start // LANE]
        pre = xb_pre[:, cols]
        sums[4:5, cols] += jnp.sum(dconv, 0, keepdims=True)
        sums[3:4, cols] += jnp.sum(dconv * pre, 0, keepdims=True)
        dpre_cols = taps[3:4, own] * dconv
        for k, ext in ((1, ext1), (2, ext2), (3, ext3)):
            ext[0:GROUP, cols] = dconv * masks[k]
            shifted = ext[k:k + GROUP, cols]
            dpre_cols = dpre_cols + taps[3 - k:4 - k, own] * shifted
            sums[3 - k:4 - k, cols] += jnp.sum(shifted * pre, 0, keepdims=True)
        dcat[:, cols] = dpre_cols.astype(bf16)
    for k, ext in enumerate((ext1, ext2, ext3)):
        edge[k * SUB:(k + 1) * SUB] = ext[0:SUB]

    grads, dz = dcat[...], dz_in[...]
    per = dh0.shape[1] // LANE
    norm_dot = jnp.zeros((GROUP, LANE), f32)
    norm_rows = jnp.zeros((SUB, LANE), f32)
    row = lax.broadcasted_iota(jnp.int32, (SUB, LANE), 0)
    for rel, dh in enumerate((dh0, dh1, dh2, dh3)):
        absolute = jnp.bitwise_xor(me, rel)
        places = [meta[1 + absolute * per + half] for half in range(per)]
        weight_x = jnp.concatenate([w_x[block_slice(place), :] for place in places], 0)
        weight_z = jnp.concatenate([w_z[block_slice(place), :] for place in places], 0)
        part = dot(grads, weight_x, 1, 1) + dot(dz, weight_z, 1, 1)
        dh[...] = part.astype(bf16)
        for half, place in enumerate(places):
            cols = slice(half * LANE, (half + 1) * LANE)
            product = part[:, cols] * hid[:, block_slice(place)].astype(f32)
            norm_dot = norm_dot + product
            norm_rows = norm_rows + jnp.where(
                row == absolute * per + half, jnp.sum(product, 0, keepdims=True), 0.0
            )
    sums[:, mixed + inner:] += norm_rows
    nd_out[0] = to_rows(jnp.sum(norm_dot, -1, keepdims=True))


def last_kernel(width, quarters, meta, gain, rs_row, nd, rows, cot, dh, *refs):
    grad = refs[-1]
    part = rows.shape[1]
    own_gain = gain[:, pl.ds(pl.multiple_of(meta[0] * part, LANE), part)]
    length = refs[0].shape[0]
    for index in range(rs_row.shape[0]):
        here = slice(index * GROUP, (index + 1) * GROUP)
        quarter, inside = divmod(index * GROUP, length)
        there = slice(inside, inside + GROUP)
        near, far = refs[quarter][there], refs[quarters + quarter][there]
        rs = to_column(rs_row[index])
        mean = to_column(nd[index]) / width
        normed = rows[here].astype(f32) * rs
        total = dh[here].astype(f32) + near.astype(f32) + far.astype(f32)
        grad[here] = (cot[here].astype(f32) + rs * (total * own_gain - normed * mean)).astype(bf16)


def smem():
    return pl.BlockSpec(memory_space=pltpu.SMEM)


def whole(array):
    zeros = (0,) * array.ndim
    return pl.BlockSpec(array.shape, lambda i: zeros)


def run(kernel, steps, ins, outs, scratch, flops, bytes_accessed, kept=None):
    kept = kept or {}
    unread = len(kept)

    def body(*refs):
        kernel(*refs[unread:])

    return pl.pallas_call(
        body,
        grid=(steps,),
        in_specs=[pl.BlockSpec(memory_space=pl.ANY)] * unread + [spec for _, spec in ins],
        out_specs=[spec for _, spec in outs],
        out_shape=[shape for shape, _ in outs],
        scratch_shapes=scratch,
        input_output_aliases={i: place for i, place in enumerate(kept)},
        compiler_params=pltpu.CompilerParams(
            vmem_limit_bytes=VMEM_LIMIT, dimension_semantics=("arbitrary",)
        ),
        cost_estimate=pl.CostEstimate(
            flops=flops, bytes_accessed=bytes_accessed, transcendentals=0
        ),
    )(*kept.values(), *[array for array, _ in ins])


def ring_order(count):
    return list(range(0, count, 2)) + list(range(count - 1 - count % 2, 0, -2))


def ring_pairs(count, shift):
    order = ring_order(count)
    return [(order[i], order[(i + shift) % count]) for i in range(count)]


def swap(array, axis, rel):
    count = lax.axis_size(axis)
    return lax.ppermute(array, axis, [(i, i ^ rel) for i in range(count)])


def ring_gather(arrays):
    count = lax.axis_size("fsdp")
    ahead, back = list(arrays), list(arrays)
    blocks = [[array] + [None] * (count - 1) for array in arrays]
    for step in range(1, count // 2 + 1):
        for i in range(len(arrays)):
            ahead[i] = blocks[i][step] = lax.ppermute(ahead[i], "fsdp", ring_pairs(count, 1))
            if step < count - step:
                back[i] = lax.ppermute(back[i], "fsdp", ring_pairs(count, -1))
                blocks[i][count - step] = back[i]
    return blocks


def ring_distance(step):
    count = lax.axis_size("fsdp")
    return {1: count // 2 - step, -1: count - 1 - count // 2 - step}


def ring_first(blocks):
    return {
        shift: blocks[(-shift * far) % len(blocks)]
        for shift, far in ring_distance(0).items() if far > 0
    }


def ring_move(blocks, step, moving, waits=()):
    onward, arrived = {}, []
    for shift, far in ring_distance(step).items():
        if far <= 0:
            continue
        got = lax.ppermute(moving[shift], "fsdp", ring_pairs(len(blocks), shift))
        if far == 1:
            arrived.append(got)
        else:
            mine = blocks[(-shift * (far - 1)) % len(blocks)]
            if waits:
                (mine,) = after((mine,), waits)
            onward[shift] = (mine.astype(f32) + got.astype(f32)).astype(bf16)
    return onward, arrived


def double_up(array, axis):
    rel = 1
    while rel < lax.axis_size(axis):
        array = array + swap(array, axis, rel)
        rel *= 2
    return array


def head_gather(own):
    far = swap(own, "head", 2)
    return [own, swap(own, "head", 1), far, swap(far, "head", 1)]


def spread_rows(rows):
    return [rows] + [swap(rows, "head", rel) for rel in (1, 2, 3)]


def after(arrays, others):
    return lax.optimization_barrier((tuple(arrays), tuple(others)))[0]


def shards(
    block_in, segment_ids, norm_gain, proj_z, proj_x, proj_bc, proj_dt, conv_x, bias_x, conv_bc,
    bias_bc, dt_bias, a_log, skip_d, gate_gain, proj_out, cotangent,
):
    seqs, seq_len = segment_ids.shape
    tokens = seqs * seq_len
    head_devs = lax.axis_size("head")
    fsdp_devs = lax.axis_size("fsdp")
    me = lax.axis_index("head")
    width_part = block_in.shape[1]
    width = width_part * head_devs
    heads = dt_bias.shape[0]
    inner = bias_x.shape[0]
    head_dim = inner // heads
    inner_full = inner * head_devs
    state_dim = conv_bc.shape[1] // 2
    mixed = inner + 2 * state_dim
    n_groups = seq_len // GROUP
    groups = seqs * n_groups
    feature_blocks = width // LANE
    ringed = fsdp_devs == feature_blocks
    back_cols = mixed + LANE

    join_ins = (proj_z, proj_out, proj_x, proj_bc, proj_dt.T)
    late_mine, early_mine = pl.pallas_call(
        functools.partial(join_kernel, LANE),
        out_shape=[
            jax.ShapeDtypeStruct((proj_z.shape[0], 2 * inner), bf16),
            jax.ShapeDtypeStruct((proj_z.shape[0], back_cols), bf16),
        ],
    )(*join_ins)
    rows_all = head_gather(block_in)
    if ringed:
        order = ring_order(fsdp_devs)
        position = np.array([order.index(i) for i in range(fsdp_devs)])
        places = (position[:, None] - position[None]) % fsdp_devs
        w_x, w_zo = [
            jnp.concatenate(blocks, 0) for blocks in ring_gather([early_mine, late_mine])
        ]
        (cot_mine,) = after((cotangent,), (rows_all[2],))
    else:
        cot_mine = cotangent
        places = np.tile(np.arange(feature_blocks), (fsdp_devs, 1))
        w_x, w_zo = [
            lax.all_gather(a, "fsdp", axis=0, tiled=True) for a in (early_mine, late_mine)
        ]
    cots = head_gather(cot_mine)
    table = np.zeros((fsdp_devs, head_devs, 1 + feature_blocks), np.int32)
    table[:, :, 0] = np.arange(head_devs)[None]
    table[:, :, 1:] = places[:, None]
    meta = lax.dynamic_index_in_dim(
        jnp.asarray(table.reshape(-1, 1 + feature_blocks)),
        lax.axis_index(("fsdp", "head")), 0, False,
    )

    head_par = jnp.pad(
        jnp.stack([dt_bias, -jnp.exp(a_log), skip_d]), ((0, SUB - 3), (0, LANE - heads))
    )
    lanes = np.arange(LANE)[:, None]
    owners = (np.arange(inner) // head_dim)[None]
    spread = jnp.asarray(((lanes % heads == owners) & (lanes < 3 * heads)), bf16)
    heads_of = jnp.asarray((lanes == owners).T, bf16)
    gain = norm_gain[None]
    gate_row = gate_gain[None]

    token_shape = lambda cols, dtype: jax.ShapeDtypeStruct((tokens, cols), dtype)
    row_shape = lambda count: jax.ShapeDtypeStruct((count, SUB, GROUP), f32)

    def part(cols, base=0, back=False):
        if back:
            return pl.BlockSpec((GROUP, cols), lambda i: (base + n_groups - 1 - i, 0))
        return pl.BlockSpec((GROUP, cols), lambda i: (base + i, 0))

    def row_part(base=0, back=False, rows=SUB, cols=GROUP):
        if back:
            return pl.BlockSpec((1, rows, cols), lambda i: (base + n_groups - 1 - i, 0, 0))
        return pl.BlockSpec((1, rows, cols), lambda i: (base + i, 0, 0))

    def z_weights(side):
        return (w_zo, pl.BlockSpec((width, inner), lambda i: (0, side)))

    def keep(earlier, count):
        return {i: earlier[i] for i in range(count)} if earlier else {}

    enter_shape = jax.ShapeDtypeStruct((groups, state_dim, inner), f32)

    def forward(s, earlier):
        base = s * n_groups
        ins = [(meta, smem())] + [(r, part(width_part, base)) for r in rows_all]
        ins += [(segment_ids, whole(segment_ids)), (w_x, whole(w_x)), z_weights(0)]
        consts = (gain, conv_x, conv_bc, bias_x[None], bias_bc[None], head_par, spread)
        ins += [(a, whole(a)) for a in consts]
        outs = [(token_shape(width, bf16), part(width, base))]
        outs += [
            (token_shape(cols, f32), part(cols, base))
            for cols in (mixed, mixed, inner, LANE, LANE, inner)
        ]
        outs += [(enter_shape, row_part(base, False, state_dim, inner))]
        outs += [(row_shape(groups), row_part(base)), (row_shape(n_groups), row_part())]
        scratch = [pltpu.VMEM((GROUP + SUB, mixed), f32), pltpu.VMEM((state_dim, inner), f32)]
        kernel = functools.partial(forward_kernel, heads, head_dim, state_dim, s)
        return run(
            kernel, n_groups, ins, outs, scratch, 25 * 10**9, 20 * 2**20, keep(earlier, 9)
        )

    wide = 2 if n_groups % 2 == 0 else 1

    def tall(cols, base=0):
        return pl.BlockSpec((wide * GROUP, cols), lambda i: (base // wide + i, 0))

    def tall_row(base=0):
        return pl.BlockSpec((wide, SUB, GROUP), lambda i: (base // wide + i, 0, 0))

    def gate(s, squares, z, y, gain_in, earlier):
        base = s * n_groups
        ins = [(meta, smem())] + [(a, tall_row()) for a in squares]
        ins += [(z, tall(inner, base)), (y, tall(inner, base))]
        ins += [(c, tall(width_part, base)) for c in cots]
        ins += [z_weights(1)] + [(a, whole(a)) for a in (gate_row, gain_in)]
        gain_shape = jax.ShapeDtypeStruct((SUB, inner), f32)
        outs = [(token_shape(width_part, bf16), tall(width_part, base))] * 4 + [
            (token_shape(inner, bf16), tall(inner, base)),
            (token_shape(inner, f32), tall(inner, base)),
            (token_shape(width, bf16), tall(width, base)),
            (row_shape(groups), tall_row(base)),
            (row_shape(groups), tall_row(base)),
            (gain_shape, whole(gain_shape)),
        ]
        kernel = functools.partial(gate_kernel, inner_full)
        return run(kernel, n_groups // wide, ins, outs, [], 12 * 10**9, 12 * 2**20, keep(earlier, 9))

    def gate_back(rs, dots, z, y, dyn):
        ins = [(a, tall_row()) for a in (rs, *dots)] + [(a, tall(inner)) for a in (z, y, dyn)]
        ins += [(gate_row, whole(gate_row))]
        outs = [(token_shape(inner, bf16), tall(inner))] * 2
        kernel = functools.partial(gate_back_kernel, inner_full)
        return run(kernel, groups // wide, ins, outs, [], 12 * 10**9, 16 * 2**20)

    quarter = wide
    quarter_rows = quarter * GROUP

    def backward(s, q, arrays, enter, hid, sums_in, earlier, waits):
        base = s * n_groups + q * quarter
        fresh = (q + 1) * quarter == n_groups

        def back_part(cols, first=base):
            return pl.BlockSpec((GROUP, cols), lambda i: (first + quarter - 1 - i, 0))

        def back_row(rows=SUB, cols=GROUP):
            return pl.BlockSpec((1, rows, cols), lambda i: (base + quarter - 1 - i, 0, 0))

        state_shape = jax.ShapeDtypeStruct((state_dim, inner), f32)
        edge_shape = jax.ShapeDtypeStruct((3 * SUB, mixed), f32)
        sums_shape = jax.ShapeDtypeStruct(sums_in.shape, f32)
        state, edge = (earlier[7], earlier[8]) if earlier else (
            jnp.zeros(state_shape.shape, f32), jnp.zeros(edge_shape.shape, f32)
        )
        ins = [(meta, smem())] + [(a, back_part(a.shape[1])) for a in arrays]
        ins += [(enter, back_row(state_dim, inner)), (hid, back_part(width))]
        ins += [(segment_ids, whole(segment_ids)), (w_x, whole(w_x)), z_weights(0)]
        (sums_in,) = after((sums_in,), waits)
        consts = (conv_x, conv_bc, head_par, spread, heads_of, sums_in, state, edge)
        ins += [(a, whole(a)) for a in consts]
        dh_shape = jax.ShapeDtypeStruct((quarter_rows, width_part), bf16)
        outs = [(token_shape(back_cols, bf16), back_part(back_cols))]
        outs += [(token_shape(width_part, bf16), back_part(width_part))]
        outs += [(row_shape(groups), back_row())]
        outs += [(dh_shape, back_part(width_part, 0))] * 3
        outs += [(a, whole(a)) for a in (sums_shape, state_shape, edge_shape)]
        scratch = [pltpu.VMEM((GROUP + SUB, mixed), f32)] * 3
        kernel = functools.partial(
            backward_kernel, heads, head_dim, state_dim, (q + 1) * quarter - 1, s, fresh
        )
        return run(
            kernel, quarter, ins, outs, scratch, 30 * 10**9, 13 * 2**20, keep(earlier, 3)
        )

    def last(first, nears, fars, nd, dh, earlier):
        count = len(nears)
        rows = count * quarter_rows
        own = pl.BlockSpec((rows, width_part), lambda i: (first // count, 0))
        own_rows = pl.BlockSpec((count * quarter, SUB, GROUP), lambda i: (first // count, 0, 0))
        ins = [(meta, smem()), (gain, whole(gain)), (norm_rs, own_rows), (nd, own_rows)]
        ins += [(a, own) for a in (block_in, cotangent, dh)]
        ins += [(a, whole(a)) for a in (*nears, *fars)]
        outs = [(token_shape(width_part, bf16), own)]
        kernel = functools.partial(last_kernel, width, count)
        return run(kernel, 1, ins, outs, [], 4 * 10**9, 4 * 2**20, keep(earlier, 1))

    def far_sum(mine, got):
        return (mine.astype(f32) + got.astype(f32)).astype(bf16)

    fwd, squares = None, []
    for s in range(seqs):
        fwd = forward(s, fwd)
        squares.append(spread_rows(fwd[9]))
    hid, xb_pre, xb_conv, z, v, cum, y, enter, norm_rs = fwd[:9]
    gates, gain_sum = None, jnp.zeros((SUB, inner), f32)
    for s in range(seqs):
        gates = gate(s, squares[s], z, y, gain_sum, gates)
        gain_sum = gates[9]
    out0, out1, out2, out3, yn, dyn, cot_whole, gate_dots, gate_rs = gates[:9]
    got1, got3 = swap(out1, "head", 1), swap(out3, "head", 1)
    dots = spread_rows(gate_dots)
    g_out = dot(cot_whole, yn, 0, 0).astype(bf16)
    out_sum = far_sum(*after((out2, got3), (got1,)))
    out_far = swap(out_sum, "head", 2)
    out_rows = (
        block_in.astype(f32) + out0.astype(f32) + got1.astype(f32) + out_far.astype(f32)
    ).astype(bf16)
    dy, dz = gate_back(gate_rs, dots, z, y, dyn)
    g_z = dot(hid, dz, 0, 0).astype(bf16)
    g_early = jnp.concatenate([g_z, g_out], 1)
    blocks = lambda a: [a[i * LANE:(i + 1) * LANE] for i in range(feature_blocks)]
    scatter = lambda a: lax.psum_scatter(
        a.astype(f32), "fsdp", scatter_dimension=0, tiled=True
    )
    moving = ring_first(blocks(g_early)) if ringed else {}
    arrived = []

    sums = jnp.pad(gain_sum[:1], ((1, SUB - 2), (mixed, LANE)))
    per_seq = n_groups // quarter
    steps = [(s, q) for s in range(seqs) for q in reversed(range(per_seq))]
    back = None
    nears, fars, far_gots = [], [], []
    for index, (s, q) in enumerate(steps):
        waits = [g_early, out_sum, *moving.values(), *fars[:index - 1], *far_gots[:max(index - 2, 0)]]
        if index >= 2:
            waits.append(out_rows)
        if index >= 1:
            waits += [nears[index - 1], fars[index - 1]]
        back = backward(
            s, q, (dy, dz, y, xb_pre, xb_conv, v, cum), enter, hid, sums, back, waits
        )
        if moving:
            moving, got = ring_move(blocks(g_early), index, moving, (back[6],))
            arrived += got
        _, dh0, nd, dh1, dh2, dh3, sums = back[:7]
        far_near = swap(dh3, "head", 1)
        nears.append(swap(dh1, "head", 1))
        fars.append(far_sum(dh2, far_near))
        far_gots.append(swap(fars[-1], "head", 2))
    (dcat,) = after((back[0],), (*fars[:-1], *far_gots[:-2], *arrived))
    g_late = dot(hid, dcat, 0, 0).astype(bf16)
    places_of = {s * per_seq + q: i for i, (s, q) in enumerate(steps)}
    near_at = [nears[places_of[i]] for i in range(len(steps))]
    far_at = [far_gots[places_of[i]] for i in range(len(steps))]

    nd = double_up(nd, "head")
    grad_rows = None
    if ringed:
        s_early = sum([a.astype(f32) for a in arrived], g_early[:LANE].astype(f32))
        moving = ring_first(blocks(g_late))
        s_late = g_late[:LANE].astype(f32)
        step = 0
        while moving:
            moving, got = ring_move(blocks(g_late), step, moving)
            s_late = sum([a.astype(f32) for a in got], s_late)
            if step == 1 and moving:
                moving = dict(zip(moving, after(moving.values(), (nd, far_gots[-1]))))
            step += 1
    else:
        s_early, s_late = scatter(g_early), scatter(g_late)
    for s in range(seqs):
        here = slice(s * per_seq, (s + 1) * per_seq)
        grad_rows = last(s * per_seq, near_at[here], far_at[here], nd, back[1], grad_rows)
    bc_part = 2 * state_dim // head_devs
    s_bc_all = s_late[:, inner:mixed].reshape(-1, head_devs, bc_part).transpose(1, 0, 2)
    s_bc = lax.dynamic_index_in_dim(s_bc_all, me, 0, False)
    for rel in (1, 2, 3):
        s_bc = s_bc + swap(lax.dynamic_index_in_dim(s_bc_all, me ^ rel, 0, False), "head", rel)

    fsdp_sums = double_up(sums, "fsdp")
    all_sums = double_up(fsdp_sums, "head")
    norm_sums = all_sums[:, mixed + inner:].reshape(head_devs, width_part) / norm_gain.reshape(
        head_devs, width_part
    )
    return (
        out_rows,
        grad_rows[0],
        lax.dynamic_index_in_dim(norm_sums, me, 0, False),
        s_early[:, :inner],
        s_late[:, :inner],
        s_bc,
        s_late[:, mixed:mixed + heads],
        fsdp_sums[:4, :inner],
        fsdp_sums[4, :inner],
        all_sums[:4, inner:mixed],
        all_sums[4, inner:mixed],
        fsdp_sums[3, mixed:mixed + heads],
        fsdp_sums[2, mixed:mixed + heads] * -jnp.exp(a_log),
        fsdp_sums[0, mixed:mixed + inner].reshape(heads, head_dim).sum(1),
        fsdp_sums[1, mixed:mixed + inner],
        s_early[:, inner:].T,
    )


def solution(mesh):
    in_specs = (
        P("fsdp", "head"), P("fsdp", None), P(), P("fsdp", "head"), P("fsdp", "head"),
        P("fsdp", None), P("fsdp", "head"), P(None, "head"), P("head"), P(), P(), P("head"),
        P("head"), P("head"), P("head"), P("head", "fsdp"), P("fsdp", "head"),
    )
    out_specs = (
        P("fsdp", "head"), P("fsdp", "head"), P("head"), P("fsdp", "head"), P("fsdp", "head"),
        P("fsdp", "head"), P("fsdp", "head"), P(None, "head"), P("head"), P(), P(), P("head"),
        P("head"), P("head"), P("head"), P("head", "fsdp"),
    )
    return jax.shard_map(shards, mesh=mesh, in_specs=in_specs, out_specs=out_specs, check_vma=False)
```

```python
import functools

import jax
import jax.numpy as jnp
import numpy as np
from jax import lax
from jax.experimental import pallas as pl
from jax.experimental.pallas import tpu as pltpu
from jax.sharding import PartitionSpec as P

GROUP = 256
LANE = 128
SUB = 8

epsilon = 1e-05
neg_big = -1e30
f32 = jnp.float32
bf16 = jnp.bfloat16

VMEM_LIMIT = 56 * 1024 * 1024


def dot(left, right, left_dim=1, right_dim=0):
    return lax.dot_general(
        left, right, (((left_dim,), (right_dim,)), ((), ())), preferred_element_type=f32
    )


def sigmoid(values):
    return 1.0 / (1.0 + jnp.exp(-values))


def softplus(values):
    return jnp.maximum(values, 0.0) + jnp.log1p(jnp.exp(-jnp.abs(values)))


def split_pack(values, count):
    high = values.astype(bf16).astype(f32)
    rest = values - high
    mid = rest.astype(bf16).astype(f32)
    last = rest - mid
    packed = high + pltpu.roll(mid, count, 1) + pltpu.roll(last, 2 * count, 1)
    return packed.astype(bf16)


def fold_lanes(values, count):
    lanes = values.shape[1]
    return values + pltpu.roll(values, lanes - count, 1) + pltpu.roll(values, lanes - 2 * count, 1)


def triangle(size, upper):
    row = lax.broadcasted_iota(jnp.int32, (size, size), 0)
    col = lax.broadcasted_iota(jnp.int32, (size, size), 1)
    return (row <= col if upper else row >= col)


def head_sums(values, heads_of):
    high = values.astype(bf16)
    low = (values - high.astype(f32)).astype(bf16)
    return dot(high, heads_of) + dot(low, heads_of)


def to_rows(column):
    wide = jnp.broadcast_to(column, (column.shape[0], LANE))
    return wide.T[:SUB]


def to_column(rows):
    return rows.T[:, :1]


def block_slice(index):
    return pl.ds(pl.multiple_of(index * LANE, LANE), LANE)


def segment_rows(seg, seq, group):
    start = pl.multiple_of(jnp.maximum(group * GROUP - LANE, 0), LANE)
    now = seg[seq:seq + 1, pl.ds(pl.multiple_of(group * GROUP, GROUP), GROUP)].astype(f32)
    old = jnp.where(group > 0, seg[seq:seq + 1, pl.ds(start, LANE)].astype(f32), -1.0)
    both = jnp.broadcast_to(jnp.concatenate([old, now], 1), (SUB, LANE + GROUP))
    end, prev = now[:, GROUP - 1:], old[:, LANE - 1:]
    now_rows = jnp.broadcast_to(now, (SUB, GROUP))
    row = lax.broadcasted_iota(jnp.int32, (SUB, GROUP), 0)
    rows = jnp.where(row == 0, now_rows, 0.0)
    for k in (1, 2, 3):
        same = pltpu.roll(both, k, 1)[:, LANE:] == now_rows
        rows = jnp.where((row == k) & same, 1.0, rows)
    rows = jnp.where((row == 4) & (now_rows == end), 1.0, rows)
    rows = jnp.where((row == 5) & (now_rows == prev), 1.0, rows)
    return now, rows.T, (end == prev).astype(f32)


def scan_terms(cum, dt, tok, link, head_par, spread, heads):
    lane = lax.broadcasted_iota(jnp.int32, (GROUP, LANE), 1)
    real = lane < heads
    end = cum[GROUP - 1:GROUP]
    ain = jnp.where(real, jnp.exp(cum) * tok[:, 5:6], 0.0)
    w_end = jnp.where(real, jnp.exp(end - cum) * tok[:, 4:5], 0.0)
    carry = jnp.where(real[:SUB], jnp.exp(jnp.broadcast_to(end, (SUB, LANE))) * link, 0.0)
    wide = dot(
        jnp.concatenate([split_pack(a, heads) for a in (dt, ain, w_end, carry, head_par)], 0),
        spread,
    )
    cuts = [wide[i * GROUP:(i + 1) * GROUP] for i in range(3)]
    carry_wide = wide[3 * GROUP:3 * GROUP + 1]
    skip = wide[3 * GROUP + SUB + 2:3 * GROUP + SUB + 3]
    return w_end, cuts, carry_wide, skip


def join_kernel(lanes, z, out, x, bc, dt, late, early):
    inner, mixed = z.shape[1], x.shape[1] + bc.shape[1]
    late[:, :inner] = z[...]
    late[:, inner:] = out[...].T
    early[:, :inner] = x[...]
    early[:, inner:mixed] = bc[...]
    early[:, mixed:] = jnp.concatenate(
        [dt[...], jnp.zeros((lanes - dt.shape[0], dt.shape[1]), bf16)], 0
    ).T


def forward_kernel(
    heads, head_dim, state_dim, first_group, seq, fresh,
    meta, row0, row1, row2, row3, seg, w_x, gain, conv_x, conv_bc, bias_x, bias_bc, head_par, spread,
    held_in, edge_in,
    hid, xb_pre, xb_conv, v_out, cum_out, y_out, enter_out, rs_out, held, edge,
    ext,
):
    inner = heads * head_dim
    mixed = inner + 2 * state_dim
    step = pl.program_id(0)
    me = meta[0]
    parts = [ref[...].astype(f32) for ref in (row0, row1, row2, row3)]
    total = sum([jnp.sum(part * part, -1, keepdims=True) for part in parts])
    width = 4 * parts[0].shape[1]
    rs = lax.rsqrt(total / width + epsilon)
    rs_out[0] = to_rows(rs)
    per = parts[0].shape[1] // LANE
    for rel in range(4):
        absolute = jnp.bitwise_xor(me, rel)
        for half in range(per):
            feature = absolute * per + half
            scale = gain[:, block_slice(feature)]
            part = parts[rel][:, half * LANE:(half + 1) * LANE]
            hid[:, block_slice(meta[1 + feature])] = (part * rs * scale).astype(bf16)
    hidden = hid[...]

    @pl.when(step == 0)
    def _():
        held[...] = jnp.zeros(held.shape, f32) if fresh else held_in[...]
        edge[...] = jnp.zeros(edge.shape, f32) if fresh else edge_in[...]

    ext[0:SUB] = edge[...]
    seg_row, tok, link = segment_rows(seg, seq, first_group + step)
    pre = dot(hidden, w_x[:, :mixed])
    ext[SUB:SUB + GROUP] = pre
    edge[...] = pre[GROUP - SUB:]
    xb_pre[...] = pre
    masks = [None] + [jnp.broadcast_to(tok[:, k:k + 1], (GROUP, LANE)) for k in (1, 2, 3)]
    acts = []
    for start in range(0, mixed, LANE):
        cols = slice(start, start + LANE)
        taps, bias = (conv_x, bias_x) if start < inner else (conv_bc, bias_bc)
        own = cols if start < inner else slice(start - inner, start - inner + LANE)
        conv = bias[:, own] + taps[3:4, own] * ext[SUB:SUB + GROUP, cols]
        for k in (1, 2, 3):
            conv = conv + taps[3 - k:4 - k, own] * (ext[SUB - k:SUB - k + GROUP, cols] * masks[k])
        xb_conv[:, cols] = conv
        acts.append((conv * sigmoid(conv)).astype(bf16))
    x = jnp.concatenate(acts[:inner // LANE], 1)
    b = jnp.concatenate(acts[inner // LANE:(inner + state_dim) // LANE], 1)
    c = jnp.concatenate(acts[(inner + state_dim) // LANE:], 1)

    lane = lax.broadcasted_iota(jnp.int32, (GROUP, LANE), 1)
    real = lane < heads
    v = dot(hidden, w_x[:, mixed:]) + head_par[0:1]
    v_out[...] = v
    dt = jnp.where(real, softplus(v), 0.0)
    tri = triangle(GROUP, False)
    tri_low = tri.astype(f32).astype(bf16)
    cum = fold_lanes(dot(tri_low, split_pack(dt * head_par[1:2], heads)), heads)
    cum = jnp.where(real, cum, 0.0)
    cum_out[...] = cum
    cum_t = cum.T
    _, (dt_wide, ain_wide, end_wide), carry_wide, skip = scan_terms(
        cum, dt, tok, link, head_par[...], spread[...], heads
    )
    x32 = x.astype(f32)
    xdt32 = x32 * dt_wide
    xdt = xdt32.astype(bf16)
    xw = (xdt32 * end_wide).astype(bf16)

    gram = dot(c, b, 1, 1)
    allowed = tri & (tok[:, 0:1] == seg_row)
    off = jnp.where(allowed, 0.0, neg_big)
    first = lane < head_dim
    entering = held[...]
    enter_out[0] = entering
    u = dot(c, entering.astype(bf16))
    zero = jnp.zeros((GROUP, LANE), bf16)
    for pair in range(heads // 2):
        cols = slice(pair * LANE, (pair + 1) * LANE)
        xp = xdt[:, cols]
        intra = 0.0
        for odd in range(2):
            head = 2 * pair + odd
            decay = jnp.exp(cum[:, head:head + 1] - cum_t[head:head + 1] + off)
            weight = (gram * decay).astype(bf16)
            mine = jnp.where(first, xp, zero) if odd == 0 else jnp.where(first, zero, xp)
            intra = intra + dot(weight, mine)
        y_out[:, cols] = intra + ain_wide[:, cols] * u[:, cols] + skip[:, cols] * x32[:, cols]
    held[...] = dot(b, xw, 0, 0) + carry_wide * entering


def gate_forward_kernel(
    meta, hid, y, w_z, w_out, cot0, cot1, cot2, cot3, gate_gain, z_out, dyn_out, cot_out, rows_out
):
    me = meta[0]
    per = cot0.shape[1] // LANE
    z = dot(hid[...], w_z[...])
    z_out[...] = z
    dyn = 0.0
    for rel, cot in enumerate((cot0, cot1, cot2, cot3)):
        absolute = jnp.bitwise_xor(me, rel)
        places = [meta[1 + absolute * per + half] for half in range(per)]
        weight = jnp.concatenate([w_out[block_slice(place), :] for place in places], 0)
        cv = cot[...]
        dyn = dyn + dot(cv, weight)
        for half, place in enumerate(places):
            cot_out[:, block_slice(place)] = cv[:, half * LANE:(half + 1) * LANE]
    dyn_out[...] = dyn
    square = jnp.zeros((z.shape[0], LANE), f32)
    gd = jnp.zeros((z.shape[0], LANE), f32)
    for start in range(0, z.shape[1], LANE):
        cols = slice(start, start + LANE)
        zc = z[:, cols]
        gated = y[:, cols] * zc * sigmoid(zc)
        square = square + gated * gated
        gd = gd + dyn[:, cols] * gate_gain[:, cols] * gated
    square = jnp.sum(square, -1, keepdims=True)
    gd = jnp.sum(gd, -1, keepdims=True)
    upper = lax.broadcasted_iota(jnp.int32, (SUB, GROUP), 0) < SUB // 2
    for i in range(rows_out.shape[0]):
        here = slice(i * GROUP, (i + 1) * GROUP)
        rows_out[i] = jnp.where(upper, to_rows(square[here]), to_rows(gd[here]))


def gate_kernel(
    inner_full,
    meta, sum0, sum1, sum2, sum3, z, y, dyn, w_out, gate_gain, gain_in,
    out0, out1, out2, out3, yn_out, dy_out, dz_out, gain_out,
):
    step = pl.program_id(0)
    me = meta[0]
    both = [
        (sum0[i] + sum1[i] + sum2[i] + sum3[i]).T for i in range(sum0.shape[0])
    ]
    square = jnp.concatenate([columns[:, :1] for columns in both], 0)
    gd = jnp.concatenate([columns[:, SUB - 1:] for columns in both], 0)
    rs = lax.rsqrt(square / inner_full + epsilon)
    inner_dot = gd * rs / inner_full

    @pl.when(step == 0)
    def _():
        gain_out[...] = gain_in[...]

    for start in range(0, z.shape[1], LANE):
        cols = slice(start, start + LANE)
        zc, yc, dc = z[:, cols], y[:, cols], dyn[:, cols]
        sg = sigmoid(zc)
        zs = zc * sg
        gnorm = yc * zs * rs
        yn_out[:, cols] = (gnorm * gate_gain[:, cols]).astype(bf16)
        gain_out[0:1, cols] += jnp.sum(dc * gnorm, 0, keepdims=True)
        dgated = rs * (dc * gate_gain[:, cols] - gnorm * inner_dot)
        dy_out[:, cols] = (dgated * zs).astype(bf16)
        dz_out[:, cols] = (dgated * yc * (sg * (1.0 + zc * (1.0 - sg)))).astype(bf16)
    yn = yn_out[...]
    per = out0.shape[1] // LANE
    for rel, out in enumerate((out0, out1, out2, out3)):
        absolute = jnp.bitwise_xor(me, rel)
        places = [meta[1 + absolute * per + half] for half in range(per)]
        weight = jnp.concatenate([w_out[block_slice(place), :] for place in places], 0)
        out[...] = dot(yn, weight, 1, 1).astype(bf16)


def backward_kernel(
    heads, head_dim, state_dim, last_group, seq, fresh,
    meta, dy_in, dz_in, y, xb_pre, xb_conv, v_in, cum_in, enter_in, hid,
    seg, w_x, w_z, conv_x, conv_bc, head_par, spread, heads_of, sums_in, dheld_in, edge_in,
    dcat, dh0, nd_out, dh1, dh2, dh3, sums, dheld, edge,
    ext1, ext2, ext3,
):
    inner = heads * head_dim
    mixed = inner + 2 * state_dim
    step = pl.program_id(0)
    group = last_group - step
    me = meta[0]

    @pl.when(step == 0)
    def _():
        dheld[...] = jnp.zeros(dheld.shape, f32) if fresh else dheld_in[...]
        edge[...] = jnp.zeros(edge.shape, f32) if fresh else edge_in[...]
        sums[...] = sums_in[...]

    for k, ext in enumerate((ext1, ext2, ext3)):
        ext[GROUP:GROUP + SUB] = edge[k * SUB:(k + 1) * SUB]

    seg_row, tok, link = segment_rows(seg, seq, group)
    dy = dy_in[...]
    dy32 = dy.astype(f32)
    acts, slopes = [], []
    for start in range(0, mixed, LANE):
        conv = xb_conv[:, start:start + LANE]
        sg = sigmoid(conv)
        acts.append((conv * sg).astype(bf16))
        slopes.append(sg * (1.0 + conv * (1.0 - sg)))
    x = jnp.concatenate(acts[:inner // LANE], 1)
    b = jnp.concatenate(acts[inner // LANE:(inner + state_dim) // LANE], 1)
    c = jnp.concatenate(acts[(inner + state_dim) // LANE:], 1)
    x32 = x.astype(f32)

    lane = lax.broadcasted_iota(jnp.int32, (GROUP, LANE), 1)
    real = lane < heads
    v = v_in[...]
    dt = jnp.where(real, softplus(v), 0.0)
    cum = cum_in[...]
    cum_t = cum.T
    w_end, (dt_wide, ain_wide, end_wide), carry_wide, skip = scan_terms(
        cum, dt, tok, link, head_par[...], spread[...], heads
    )
    xdt32 = x32 * dt_wide
    xdt = xdt32.astype(bf16)
    xw = (xdt32 * end_wide).astype(bf16)

    entering = enter_in[0]
    enter_low = entering.astype(bf16)
    dstate = dheld[...]
    dstate_low = dstate.astype(bf16)
    dyw = (dy32 * ain_wide).astype(bf16)
    dc = dot(dyw, enter_low, 1, 1)
    db = dot(xw, dstate_low, 1, 1)
    bd = dot(b, dstate_low)
    gain_sum = jnp.sum(dstate * entering, 0, keepdims=True) * carry_wide
    dheld[...] = dot(c, dyw, 0, 0) + carry_wide * dstate

    gram_t = dot(b, c, 1, 1)
    tri_up = triangle(GROUP, True)
    off = jnp.where(tri_up & (tok[:, 0:1] == seg_row), 0.0, neg_big)
    first = lane < head_dim
    zero = jnp.zeros((GROUP, LANE), bf16)
    dgram_t = jnp.zeros((GROUP, GROUP), f32)
    flow, through = [], []
    for pair in range(heads // 2):
        cols = slice(pair * LANE, (pair + 1) * LANE)
        xp, dyp = xdt[:, cols], dy[:, cols]
        dxw = 0.0
        for odd in range(2):
            head = 2 * pair + odd
            decay = jnp.exp(cum_t[head:head + 1] - cum[:, head:head + 1] + off)
            weight = (gram_t * decay).astype(bf16)
            own_dy = jnp.where(first, dyp, zero) if odd == 0 else jnp.where(first, zero, dyp)
            own_x = jnp.where(first, xp, zero) if odd == 0 else jnp.where(first, zero, xp)
            dxw = dxw + dot(weight, own_dy)
            dgram_t = dgram_t + dot(own_x, dyp, 1, 1) * decay
        x_cols, dy_cols = x32[:, cols], dy32[:, cols]
        ymix = y[:, cols] - skip[:, cols] * x_cols
        flow.append(dy_cols * ymix - xp.astype(f32) * dxw)
        through.append(dxw + end_wide[:, cols] * bd[:, cols])
        sums[0:1, mixed + pair * LANE:mixed + (pair + 1) * LANE] += jnp.sum(
            dy_cols * x_cols, 0, keepdims=True
        )
    dgram_low = dgram_t.astype(bf16)
    db = db + dot(dgram_low, c)
    dc = dc + dot(dgram_low, b, 0, 0)
    q = jnp.concatenate(through, 1)
    flow_sum = head_sums(jnp.concatenate(flow, 1), heads_of[...])
    ddt = head_sums(x32 * q, heads_of[...])
    dv = head_sums(x32 * bd, heads_of[...])
    dw = dv * w_end * dt
    carried = head_sums(jnp.broadcast_to(gain_sum, (SUB, inner)), heads_of[...])[0:1]
    constant = jnp.sum(dw, 0, keepdims=True) + carried
    up = tri_up.astype(f32).astype(bf16)
    inward = jnp.where(real, flow_sum - dw, 0.0)
    dstep = fold_lanes(dot(up, split_pack(inward, heads)), heads) + constant
    dstep = jnp.where(real, dstep, 0.0)
    ddt = ddt + dstep * head_par[1:2]
    dpre = jnp.where(real, ddt * sigmoid(v), 0.0)
    sums[2:3, mixed:mixed + LANE] += jnp.sum(dstep * dt, 0, keepdims=True)
    sums[3:4, mixed:mixed + LANE] += jnp.sum(dpre, 0, keepdims=True)
    dcat[:, mixed:] = dpre.astype(bf16)

    masks = [None] + [jnp.broadcast_to(tok[:, k:k + 1], (GROUP, LANE)) for k in (1, 2, 3)]
    for start in range(0, mixed, LANE):
        cols = slice(start, start + LANE)
        taps = conv_x if start < inner else conv_bc
        own = cols if start < inner else slice(start - inner, start - inner + LANE)
        if start < inner:
            dact = dt_wide[:, cols] * q[:, cols] + skip[:, cols] * dy32[:, cols]
        elif start < inner + state_dim:
            dact = db[:, start - inner:start - inner + LANE]
        else:
            dact = dc[:, start - inner - state_dim:start - inner - state_dim + LANE]
        dconv = dact * slopes[start // LANE]
        pre = xb_pre[:, cols]
        sums[4:5, cols] += jnp.sum(dconv, 0, keepdims=True)
        sums[3:4, cols] += jnp.sum(dconv * pre, 0, keepdims=True)
        dpre_cols = taps[3:4, own] * dconv
        for k, ext in ((1, ext1), (2, ext2), (3, ext3)):
            ext[0:GROUP, cols] = dconv * masks[k]
            shifted = ext[k:k + GROUP, cols]
            dpre_cols = dpre_cols + taps[3 - k:4 - k, own] * shifted
            sums[3 - k:4 - k, cols] += jnp.sum(shifted * pre, 0, keepdims=True)
        dcat[:, cols] = dpre_cols.astype(bf16)
    for k, ext in enumerate((ext1, ext2, ext3)):
        edge[k * SUB:(k + 1) * SUB] = ext[0:SUB]

    grads, dz = dcat[...], dz_in[...]
    per = dh0.shape[1] // LANE
    norm_dot = jnp.zeros((GROUP, LANE), f32)
    norm_rows = jnp.zeros((SUB, LANE), f32)
    row = lax.broadcasted_iota(jnp.int32, (SUB, LANE), 0)
    for rel, dh in enumerate((dh0, dh1, dh2, dh3)):
        absolute = jnp.bitwise_xor(me, rel)
        places = [meta[1 + absolute * per + half] for half in range(per)]
        weight_x = jnp.concatenate([w_x[block_slice(place), :] for place in places], 0)
        weight_z = jnp.concatenate([w_z[block_slice(place), :] for place in places], 0)
        part = dot(grads, weight_x, 1, 1) + dot(dz, weight_z, 1, 1)
        dh[...] = part.astype(bf16)
        for half, place in enumerate(places):
            cols = slice(half * LANE, (half + 1) * LANE)
            product = part[:, cols] * hid[:, block_slice(place)].astype(f32)
            norm_dot = norm_dot + product
            norm_rows = norm_rows + jnp.where(
                row == absolute * per + half, jnp.sum(product, 0, keepdims=True), 0.0
            )
    sums[:, mixed + inner:] += norm_rows
    nd_out[0] = to_rows(jnp.sum(norm_dot, -1, keepdims=True))


def last_kernel(width, counts, meta, gain, rs_row, nd, rows, cot, dh, *refs):
    grad = refs[-1]
    part = rows.shape[1]
    own_gain = gain[:, pl.ds(pl.multiple_of(meta[0] * part, LANE), part)]
    length = refs[0].shape[0]
    starts = [sum(counts[:i]) for i in range(len(counts))]
    for index in range(rs_row.shape[0]):
        here = slice(index * GROUP, (index + 1) * GROUP)
        quarter, inside = divmod(index * GROUP, length)
        there = slice(inside, inside + GROUP)
        rs = to_column(rs_row[index])
        mean = to_column(nd[index]) / width
        normed = rows[here].astype(f32) * rs
        total = dh[here].astype(f32)
        for piece in refs[starts[quarter]:starts[quarter] + counts[quarter]]:
            total = total + piece[there].astype(f32)
        grad[here] = (cot[here].astype(f32) + rs * (total * own_gain - normed * mean)).astype(bf16)


def smem():
    return pl.BlockSpec(memory_space=pltpu.SMEM)


def whole(array):
    zeros = (0,) * array.ndim
    return pl.BlockSpec(array.shape, lambda i: zeros)


def run(kernel, steps, ins, outs, scratch, flops, bytes_accessed, kept=None):
    kept = kept or {}
    unread = len(kept)

    def body(*refs):
        kernel(*refs[unread:])

    return pl.pallas_call(
        body,
        grid=(steps,),
        in_specs=[pl.BlockSpec(memory_space=pl.ANY)] * unread + [spec for _, spec in ins],
        out_specs=[spec for _, spec in outs],
        out_shape=[shape for shape, _ in outs],
        scratch_shapes=scratch,
        input_output_aliases={i: place for i, place in enumerate(kept)},
        compiler_params=pltpu.CompilerParams(
            vmem_limit_bytes=VMEM_LIMIT, dimension_semantics=("arbitrary",)
        ),
        cost_estimate=pl.CostEstimate(
            flops=flops, bytes_accessed=bytes_accessed, transcendentals=0
        ),
    )(*kept.values(), *[array for array, _ in ins])


def ring_order(count):
    return list(range(0, count, 2)) + list(range(count - 1 - count % 2, 0, -2))


def ring_pairs(count, shift):
    order = ring_order(count)
    return [(order[i], order[(i + shift) % count]) for i in range(count)]


def swap(array, axis, rel):
    count = lax.axis_size(axis)
    return lax.ppermute(array, axis, [(i, i ^ rel) for i in range(count)])


def ring_hand_on(blocks, step, ends):
    count = len(blocks)
    ahead, back = ends
    ahead = blocks[step] = lax.ppermute(ahead, "fsdp", ring_pairs(count, 1))
    if step < count - step:
        back = blocks[count - step] = lax.ppermute(back, "fsdp", ring_pairs(count, -1))
    return ahead, back


def ring_distance(step):
    count = lax.axis_size("fsdp")
    return {1: count // 2 - step, -1: count - 1 - count // 2 - step}


def ring_first(blocks):
    return {
        shift: blocks[(-shift * far) % len(blocks)]
        for shift, far in ring_distance(0).items() if far > 0
    }


def ring_move(blocks, step, moving, waits=()):
    onward, arrived = {}, []
    for shift, far in ring_distance(step).items():
        if far <= 0:
            continue
        got = lax.ppermute(moving[shift], "fsdp", ring_pairs(len(blocks), shift))
        if far == 1:
            arrived.append(got)
        else:
            mine = blocks[(-shift * (far - 1)) % len(blocks)]
            if waits:
                (mine,) = after((mine,), waits)
            onward[shift] = (mine.astype(f32) + got.astype(f32)).astype(bf16)
    return onward, arrived


def double_up(array, axis):
    rel = 1
    while rel < lax.axis_size(axis):
        array = array + swap(array, axis, rel)
        rel *= 2
    return array


def head_gather(own):
    far = swap(own, "head", 2)
    return [own, swap(own, "head", 1), far, swap(far, "head", 1)]


def spread_rows(rows):
    return [rows] + [swap(rows, "head", rel) for rel in (1, 2, 3)]


def after(arrays, others):
    return lax.optimization_barrier((tuple(arrays), tuple(others)))[0]


def shards(
    block_in, segment_ids, norm_gain, proj_z, proj_x, proj_bc, proj_dt, conv_x, bias_x, conv_bc,
    bias_bc, dt_bias, a_log, skip_d, gate_gain, proj_out, cotangent,
):
    seqs, seq_len = segment_ids.shape
    tokens = seqs * seq_len
    head_devs = lax.axis_size("head")
    fsdp_devs = lax.axis_size("fsdp")
    me = lax.axis_index("head")
    width_part = block_in.shape[1]
    width = width_part * head_devs
    heads = dt_bias.shape[0]
    inner = bias_x.shape[0]
    head_dim = inner // heads
    inner_full = inner * head_devs
    state_dim = conv_bc.shape[1] // 2
    mixed = inner + 2 * state_dim
    n_groups = seq_len // GROUP
    groups = seqs * n_groups
    feature_blocks = width // LANE
    ringed = fsdp_devs == feature_blocks
    back_cols = mixed + LANE

    join_ins = (proj_z, proj_out, proj_x, proj_bc, proj_dt.T)
    late_mine, early_mine = pl.pallas_call(
        functools.partial(join_kernel, LANE),
        out_shape=[
            jax.ShapeDtypeStruct((proj_z.shape[0], 2 * inner), bf16),
            jax.ShapeDtypeStruct((proj_z.shape[0], back_cols), bf16),
        ],
    )(*join_ins)
    rows_all = head_gather(block_in)
    late_blocks = [late_mine] + [None] * (fsdp_devs - 1)
    if ringed:
        order = ring_order(fsdp_devs)
        position = np.array([order.index(i) for i in range(fsdp_devs)])
        places = (position[:, None] - position[None]) % fsdp_devs
        early_blocks = [early_mine] + [None] * (fsdp_devs - 1)
        ends = (early_mine, early_mine)
        for step in range(1, fsdp_devs // 2 + 1):
            ends = ring_hand_on(early_blocks, step, ends)
        w_x = jnp.concatenate(early_blocks, 0)
        (cot_mine,) = after((cotangent,), (rows_all[2],))
        cot_far = swap(cot_mine, "head", 2)
    else:
        cot_far = swap(cotangent, "head", 2)
        places = np.tile(np.arange(feature_blocks), (fsdp_devs, 1))
        w_x, w_zo = [
            lax.all_gather(a, "fsdp", axis=0, tiled=True) for a in (early_mine, late_mine)
        ]
    table = np.zeros((fsdp_devs, head_devs, 1 + feature_blocks), np.int32)
    table[:, :, 0] = np.arange(head_devs)[None]
    table[:, :, 1:] = places[:, None]
    meta = lax.dynamic_index_in_dim(
        jnp.asarray(table.reshape(-1, 1 + feature_blocks)),
        lax.axis_index(("fsdp", "head")), 0, False,
    )

    head_par = jnp.pad(
        jnp.stack([dt_bias, -jnp.exp(a_log), skip_d]), ((0, SUB - 3), (0, LANE - heads))
    )
    lanes = np.arange(LANE)[:, None]
    owners = (np.arange(inner) // head_dim)[None]
    spread = jnp.asarray(((lanes % heads == owners) & (lanes < 3 * heads)), bf16)
    heads_of = jnp.asarray((lanes == owners).T, bf16)
    gain = norm_gain[None]
    gate_row = gate_gain[None]

    token_shape = lambda cols, dtype: jax.ShapeDtypeStruct((tokens, cols), dtype)
    row_shape = lambda count: jax.ShapeDtypeStruct((count, SUB, GROUP), f32)

    def keep(earlier, count):
        return {i: earlier[i] for i in range(count)} if earlier else {}

    enter_shape = jax.ShapeDtypeStruct((groups, state_dim, inner), f32)

    wide = 2 if n_groups % 2 == 0 else 1
    quarter = wide
    quarter_rows = quarter * GROUP
    per_seq = n_groups // quarter
    state_shape = jax.ShapeDtypeStruct((state_dim, inner), f32)

    def z_weights(side):
        return (w_zo, pl.BlockSpec((width, inner), lambda i: (0, side)))

    def forward(s, q, earlier, waits):
        base = s * n_groups + q * quarter
        part = lambda cols: pl.BlockSpec((GROUP, cols), lambda i: (base + i, 0))
        row = lambda rows, cols: pl.BlockSpec((1, rows, cols), lambda i: (base + i, 0, 0))
        edge_shape = jax.ShapeDtypeStruct((SUB, mixed), f32)
        state, edge = (earlier[8], earlier[9]) if earlier else (
            jnp.zeros(state_shape.shape, f32), jnp.zeros(edge_shape.shape, f32)
        )
        (state,) = after((state,), waits)
        ins = [(meta, smem())] + [(r, part(width_part)) for r in rows_all]
        consts = (
            segment_ids, w_x, gain, conv_x, conv_bc, bias_x[None], bias_bc[None], head_par, spread,
            state, edge,
        )
        ins += [(a, whole(a)) for a in consts]
        outs = [(token_shape(width, bf16), part(width))]
        outs += [
            (token_shape(cols, f32), part(cols)) for cols in (mixed, mixed, LANE, LANE, inner)
        ]
        outs += [(enter_shape, row(state_dim, inner)), (row_shape(groups), row(SUB, GROUP))]
        outs += [(a, whole(a)) for a in (state_shape, edge_shape)]
        scratch = [pltpu.VMEM((GROUP + SUB, mixed), f32)]
        kernel = functools.partial(
            forward_kernel, heads, head_dim, state_dim, q * quarter, s, q == 0
        )
        return run(
            kernel, quarter, ins, outs, scratch, 16 * 10**9, 10 * 2**20, keep(earlier, 8)
        )

    def tall(cols, base=0):
        return pl.BlockSpec((wide * GROUP, cols), lambda i: (base // wide + i, 0))

    def tall_row(base=0):
        return pl.BlockSpec((wide, SUB, GROUP), lambda i: (base // wide + i, 0, 0))

    def gate_forward(s, hid, y, earlier):
        base = s * n_groups
        ins = [(meta, smem()), (hid, tall(width, base)), (y, tall(inner, base))]
        ins += [z_weights(0), z_weights(1)]
        ins += [(c, tall(width_part, base)) for c in cots] + [(gate_row, whole(gate_row))]
        outs = [(token_shape(inner, f32), tall(inner, base))] * 2
        outs += [(token_shape(width, bf16), tall(width, base)), (row_shape(n_groups), tall_row())]
        return run(
            gate_forward_kernel, n_groups // wide, ins, outs, [], 8 * 10**9, 12 * 2**20,
            keep(earlier, 3),
        )

    def gate(s, totals, z, y, dyn, gain_in, earlier):
        base = s * n_groups
        ins = [(meta, smem())] + [(a, tall_row()) for a in totals]
        ins += [(a, tall(inner, base)) for a in (z, y, dyn)]
        ins += [z_weights(1)] + [(a, whole(a)) for a in (gate_row, gain_in)]
        gain_shape = jax.ShapeDtypeStruct((SUB, inner), f32)
        outs = [(token_shape(width_part, bf16), tall(width_part, base))] * 4
        outs += [(token_shape(inner, bf16), tall(inner, base))] * 3
        outs += [(gain_shape, whole(gain_shape))]
        kernel = functools.partial(gate_kernel, inner_full)
        return run(kernel, n_groups // wide, ins, outs, [], 10 * 10**9, 12 * 2**20, keep(earlier, 7))

    def backward(s, q, arrays, enter, hid, sums_in, earlier, waits):
        base = s * n_groups + q * quarter
        fresh = (q + 1) * quarter == n_groups

        def back_part(cols, first=base):
            return pl.BlockSpec((GROUP, cols), lambda i: (first + quarter - 1 - i, 0))

        def back_row(rows=SUB, cols=GROUP):
            return pl.BlockSpec((1, rows, cols), lambda i: (base + quarter - 1 - i, 0, 0))

        edge_shape = jax.ShapeDtypeStruct((3 * SUB, mixed), f32)
        sums_shape = jax.ShapeDtypeStruct(sums_in.shape, f32)
        state, edge = (earlier[7], earlier[8]) if earlier else (
            jnp.zeros(state_shape.shape, f32), jnp.zeros(edge_shape.shape, f32)
        )
        ins = [(meta, smem())] + [(a, back_part(a.shape[1])) for a in arrays]
        ins += [(enter, back_row(state_dim, inner)), (hid, back_part(width))]
        ins += [(segment_ids, whole(segment_ids)), (w_x, whole(w_x)), z_weights(0)]
        (sums_in,) = after((sums_in,), waits)
        consts = (conv_x, conv_bc, head_par, spread, heads_of, sums_in, state, edge)
        ins += [(a, whole(a)) for a in consts]
        dh_shape = jax.ShapeDtypeStruct((quarter_rows, width_part), bf16)
        outs = [(token_shape(back_cols, bf16), back_part(back_cols))]
        outs += [(token_shape(width_part, bf16), back_part(width_part))]
        outs += [(row_shape(groups), back_row())]
        outs += [(dh_shape, back_part(width_part, 0))] * 3
        outs += [(a, whole(a)) for a in (sums_shape, state_shape, edge_shape)]
        scratch = [pltpu.VMEM((GROUP + SUB, mixed), f32)] * 3
        kernel = functools.partial(
            backward_kernel, heads, head_dim, state_dim, (q + 1) * quarter - 1, s, fresh
        )
        return run(
            kernel, quarter, ins, outs, scratch, 30 * 10**9, 13 * 2**20, keep(earlier, 3)
        )

    def last(nears, fars, dots, dh):
        pieces = [[near, *(far if isinstance(far, list) else [far])] for near, far in zip(nears, fars)]
        arrays = [meta, gain, norm_rs, *dots, block_in, cotangent, dh, *sum(pieces, [])]
        ins = [(a, whole(a)) for a in arrays]
        ins[0] = (meta, smem())
        shape = token_shape(width_part, bf16)
        counts = tuple(len(piece) for piece in pieces)
        kernel = functools.partial(last_kernel, width, counts)
        return run(kernel, 1, ins, [(shape, whole(shape))], [], 4 * 10**9, 8 * 2**20)[0]

    def far_sum(mine, got):
        return (mine.astype(f32) + got.astype(f32)).astype(bf16)

    fwd = None
    steps = [(s, q) for s in range(seqs) for q in range(per_seq)]
    ends = (late_mine, late_mine)
    if ringed:
        ends = after(ends, (w_x,))
    for index, (s, q) in enumerate(steps):
        waits = tuple(ends) if ringed else ()
        if ringed and index < fsdp_devs // 2:
            ends = ring_hand_on(late_blocks, index + 1, ends)
        fwd = forward(s, q, fwd, waits)
        if ringed:
            ends = after(ends, (fwd[8],))
        if index == len(steps) // 2:
            near_cot, far_cot = after((cotangent, cot_far), (fwd[8],))
            cots = [cotangent, swap(near_cot, "head", 1), cot_far, swap(far_cot, "head", 1)]
    hid, xb_pre, xb_conv, v, cum, y, enter, norm_rs = fwd[:8]
    if ringed:
        w_zo = jnp.concatenate(late_blocks, 0)
    gate_fwd, totals = None, []
    for s in range(seqs):
        gate_fwd = gate_forward(s, hid, y, gate_fwd)
        totals.append(spread_rows(gate_fwd[3]))
    z, dyn, cot_whole = gate_fwd[:3]
    gates, gain_sum = None, jnp.zeros((SUB, inner), f32)
    for s in range(seqs):
        gates = gate(s, totals[s], z, y, dyn, gain_sum, gates)
        gain_sum = gates[7]
    out0, out1, out2, out3, yn, dy, dz = gates[:7]
    got1, got3 = swap(out1, "head", 1), swap(out3, "head", 1)
    g_out = dot(cot_whole, yn, 0, 0).astype(bf16)
    out_sum = far_sum(*after((out2, got3), (got1,)))
    out_far = swap(out_sum, "head", 2)
    out_rows = (
        block_in.astype(f32) + out0.astype(f32) + got1.astype(f32) + out_far.astype(f32)
    ).astype(bf16)
    g_z = dot(hid, dz, 0, 0).astype(bf16)
    g_early = jnp.concatenate([g_z, g_out], 1)
    (g_early,) = after((g_early,), (out_sum,))
    blocks = lambda a: [a[i * LANE:(i + 1) * LANE] for i in range(feature_blocks)]
    scatter = lambda a: lax.psum_scatter(
        a.astype(f32), "fsdp", scatter_dimension=0, tiled=True
    )
    moving = ring_first(blocks(g_early)) if ringed else {}
    arrived = []

    sums = jnp.pad(gain_sum[:1], ((1, SUB - 2), (mixed, LANE)))
    steps = [(s, q) for s in range(seqs) for q in reversed(range(per_seq))]
    back = None
    nears, far_gots, pair = [], [], None
    for index, (s, q) in enumerate(steps):
        waits = [g_early, out_sum, *moving.values(), *nears[:max(index - 1, 0)]]
        waits += far_gots[:max(index - 2, 0)]
        if index >= 2:
            waits.append(out_rows)
        back = backward(
            s, q, (dy, dz, y, xb_pre, xb_conv, v, cum), enter, hid, sums, back, waits
        )
        _, dh0, nd, dh1, dh2, dh3, sums = back[:7]
        if pair:
            far = far_sum(*after(pair, (sums,)))
            far_gots.append(swap(far, "head", 2))
        if moving:
            moving, got = ring_move(blocks(g_early), index, moving, (sums,))
            arrived += got
        nears.append(swap(dh1, "head", 1))
        pair = None
        if index + 1 < len(steps):
            pair = (dh2, swap(dh3, "head", 1))
    far_gots.append([swap(dh2, "head", 2), swap(dh3, "head", 3)])
    (dcat,) = after((back[0],), (*nears[:-1], *far_gots[:-2], *arrived, far))
    g_late = dot(hid, dcat, 0, 0).astype(bf16)
    places_of = {s * per_seq + q: i for i, (s, q) in enumerate(steps)}
    near_at = [nears[places_of[i]] for i in range(len(steps))]
    far_at = [far_gots[places_of[i]] for i in range(len(steps))]

    def finish(dots):
        return last(near_at, far_at, dots, back[1])

    if ringed:
        s_early = sum([a.astype(f32) for a in arrived], g_early[:LANE].astype(f32))
        moving = ring_first(blocks(g_late))
        s_late = g_late[:LANE].astype(f32)
        for step in range(fsdp_devs // 2):
            moving, got = ring_move(blocks(g_late), step, moving)
            s_late = sum([a.astype(f32) for a in got], s_late)
            if step == 0:
                nd, sums = after((nd, sums), tuple(moving.values()))
                dots = (double_up(nd, "head"),)
            if step == min(1, fsdp_devs // 2 - 1):
                pieces = (*dots, *far_gots[-1], far_gots[-2], nears[-1])
                grad_rows = finish(dots)
                if moving:
                    moving = dict(zip(moving, after(moving.values(), pieces)))
            if step == 2 and moving:
                moving = dict(zip(moving, after(moving.values(), (grad_rows,))))
    else:
        s_early, s_late = scatter(g_early), scatter(g_late)
        grad_rows = finish((double_up(nd, "head"),))
    bc_part = 2 * state_dim // head_devs
    s_bc_all = s_late[:, inner:mixed].reshape(-1, head_devs, bc_part).transpose(1, 0, 2)
    s_bc = lax.dynamic_index_in_dim(s_bc_all, me, 0, False)
    for rel in (1, 2, 3):
        s_bc = s_bc + swap(lax.dynamic_index_in_dim(s_bc_all, me ^ rel, 0, False), "head", rel)

    fsdp_sums = double_up(sums, "fsdp")
    all_sums = double_up(fsdp_sums, "head")
    norm_sums = all_sums[:, mixed + inner:].reshape(head_devs, width_part) / norm_gain.reshape(
        head_devs, width_part
    )
    return (
        out_rows,
        grad_rows,
        lax.dynamic_index_in_dim(norm_sums, me, 0, False),
        s_early[:, :inner],
        s_late[:, :inner],
        s_bc,
        s_late[:, mixed:mixed + heads],
        fsdp_sums[:4, :inner],
        fsdp_sums[4, :inner],
        all_sums[:4, inner:mixed],
        all_sums[4, inner:mixed],
        fsdp_sums[3, mixed:mixed + heads],
        fsdp_sums[2, mixed:mixed + heads] * -jnp.exp(a_log),
        fsdp_sums[0, mixed:mixed + inner].reshape(heads, head_dim).sum(1),
        fsdp_sums[1, mixed:mixed + inner],
        s_early[:, inner:].T,
    )


def solution(mesh):
    in_specs = (
        P("fsdp", "head"), P("fsdp", None), P(), P("fsdp", "head"), P("fsdp", "head"),
        P("fsdp", None), P("fsdp", "head"), P(None, "head"), P("head"), P(), P(), P("head"),
        P("head"), P("head"), P("head"), P("head", "fsdp"), P("fsdp", "head"),
    )
    out_specs = (
        P("fsdp", "head"), P("fsdp", "head"), P("head"), P("fsdp", "head"), P("fsdp", "head"),
        P("fsdp", "head"), P("fsdp", "head"), P(None, "head"), P("head"), P(), P(), P("head"),
        P("head"), P("head"), P("head"), P("head", "fsdp"),
    )
    return jax.shard_map(shards, mesh=mesh, in_specs=in_specs, out_specs=out_specs, check_vma=False)
```

```python
import functools

import jax
import jax.numpy as jnp
import numpy as np
from jax import lax
from jax.experimental import pallas as pl
from jax.experimental.pallas import tpu as pltpu
from jax.sharding import PartitionSpec as P

GROUP = 256
LANE = 128
SUB = 8

epsilon = 1e-05
neg_big = -1e30
f32 = jnp.float32
bf16 = jnp.bfloat16

VMEM_LIMIT = 56 * 1024 * 1024


def dot(left, right, left_dim=1, right_dim=0):
    return lax.dot_general(
        left, right, (((left_dim,), (right_dim,)), ((), ())), preferred_element_type=f32
    )


def sigmoid(values):
    return 1.0 / (1.0 + jnp.exp(-values))


def softplus(values):
    return jnp.maximum(values, 0.0) + jnp.log1p(jnp.exp(-jnp.abs(values)))


def split_pack(values, count):
    high = values.astype(bf16).astype(f32)
    rest = values - high
    mid = rest.astype(bf16).astype(f32)
    last = rest - mid
    packed = high + pltpu.roll(mid, count, 1) + pltpu.roll(last, 2 * count, 1)
    return packed.astype(bf16)


def fold_lanes(values, count):
    lanes = values.shape[1]
    return values + pltpu.roll(values, lanes - count, 1) + pltpu.roll(values, lanes - 2 * count, 1)


def triangle(size, upper):
    row = lax.broadcasted_iota(jnp.int32, (size, size), 0)
    col = lax.broadcasted_iota(jnp.int32, (size, size), 1)
    return (row <= col if upper else row >= col)


def head_sums(values, heads_of):
    high = values.astype(bf16)
    low = (values - high.astype(f32)).astype(bf16)
    return dot(high, heads_of) + dot(low, heads_of)


def to_rows(column):
    wide = jnp.broadcast_to(column, (column.shape[0], LANE))
    return wide.T[:SUB]


def to_column(rows):
    return rows.T[:, :1]


def block_slice(index):
    return pl.ds(pl.multiple_of(index * LANE, LANE), LANE)


def segment_rows(seg, seq, group):
    start = pl.multiple_of(jnp.maximum(group * GROUP - LANE, 0), LANE)
    now = seg[seq:seq + 1, pl.ds(pl.multiple_of(group * GROUP, GROUP), GROUP)].astype(f32)
    old = jnp.where(group > 0, seg[seq:seq + 1, pl.ds(start, LANE)].astype(f32), -1.0)
    both = jnp.broadcast_to(jnp.concatenate([old, now], 1), (SUB, LANE + GROUP))
    end, prev = now[:, GROUP - 1:], old[:, LANE - 1:]
    now_rows = jnp.broadcast_to(now, (SUB, GROUP))
    row = lax.broadcasted_iota(jnp.int32, (SUB, GROUP), 0)
    rows = jnp.where(row == 0, now_rows, 0.0)
    for k in (1, 2, 3):
        same = pltpu.roll(both, k, 1)[:, LANE:] == now_rows
        rows = jnp.where((row == k) & same, 1.0, rows)
    rows = jnp.where((row == 4) & (now_rows == end), 1.0, rows)
    rows = jnp.where((row == 5) & (now_rows == prev), 1.0, rows)
    return now, rows.T, (end == prev).astype(f32)


def scan_terms(cum, dt, tok, link, head_par, spread, heads):
    lane = lax.broadcasted_iota(jnp.int32, (GROUP, LANE), 1)
    real = lane < heads
    end = cum[GROUP - 1:GROUP]
    ain = jnp.where(real, jnp.exp(cum) * tok[:, 5:6], 0.0)
    w_end = jnp.where(real, jnp.exp(end - cum) * tok[:, 4:5], 0.0)
    carry = jnp.where(real[:SUB], jnp.exp(jnp.broadcast_to(end, (SUB, LANE))) * link, 0.0)
    wide = dot(
        jnp.concatenate([split_pack(a, heads) for a in (dt, ain, w_end, carry, head_par)], 0),
        spread,
    )
    cuts = [wide[i * GROUP:(i + 1) * GROUP] for i in range(3)]
    carry_wide = wide[3 * GROUP:3 * GROUP + 1]
    skip = wide[3 * GROUP + SUB + 2:3 * GROUP + SUB + 3]
    return w_end, cuts, carry_wide, skip


def join_kernel(lanes, z, out, x, bc, dt, late, early):
    inner, mixed = z.shape[1], x.shape[1] + bc.shape[1]
    late[:, :inner] = z[...]
    late[:, inner:] = out[...].T
    early[:, :inner] = x[...]
    early[:, inner:mixed] = bc[...]
    early[:, mixed:] = jnp.concatenate(
        [dt[...], jnp.zeros((lanes - dt.shape[0], dt.shape[1]), bf16)], 0
    ).T


def forward_kernel(
    heads, head_dim, state_dim, first_group, seq, fresh,
    meta, row0, row1, row2, row3, seg, w_x, gain, conv_x, conv_bc, bias_x, bias_bc, head_par, spread,
    held_in, edge_in,
    hid, xb_pre, xb_conv, v_out, cum_out, y_out, enter_out, rs_out, held, edge,
    ext,
):
    inner = heads * head_dim
    mixed = inner + 2 * state_dim
    step = pl.program_id(0)
    me = meta[0]
    parts = [ref[...].astype(f32) for ref in (row0, row1, row2, row3)]
    total = sum([jnp.sum(part * part, -1, keepdims=True) for part in parts])
    width = 4 * parts[0].shape[1]
    rs = lax.rsqrt(total / width + epsilon)
    rs_out[0] = to_rows(rs)
    per = parts[0].shape[1] // LANE
    for rel in range(4):
        absolute = jnp.bitwise_xor(me, rel)
        for half in range(per):
            feature = absolute * per + half
            scale = gain[:, block_slice(feature)]
            part = parts[rel][:, half * LANE:(half + 1) * LANE]
            hid[:, block_slice(meta[1 + feature])] = (part * rs * scale).astype(bf16)
    hidden = hid[...]

    @pl.when(step == 0)
    def _():
        held[...] = jnp.zeros(held.shape, f32) if fresh else held_in[...]
        edge[...] = jnp.zeros(edge.shape, f32) if fresh else edge_in[...]

    ext[0:SUB] = edge[...]
    seg_row, tok, link = segment_rows(seg, seq, first_group + step)
    pre = dot(hidden, w_x[:, :mixed])
    ext[SUB:SUB + GROUP] = pre
    edge[...] = pre[GROUP - SUB:]
    xb_pre[...] = pre
    masks = [None] + [jnp.broadcast_to(tok[:, k:k + 1], (GROUP, LANE)) for k in (1, 2, 3)]
    acts = []
    for start in range(0, mixed, LANE):
        cols = slice(start, start + LANE)
        taps, bias = (conv_x, bias_x) if start < inner else (conv_bc, bias_bc)
        own = cols if start < inner else slice(start - inner, start - inner + LANE)
        conv = bias[:, own] + taps[3:4, own] * ext[SUB:SUB + GROUP, cols]
        for k in (1, 2, 3):
            conv = conv + taps[3 - k:4 - k, own] * (ext[SUB - k:SUB - k + GROUP, cols] * masks[k])
        xb_conv[:, cols] = conv
        acts.append((conv * sigmoid(conv)).astype(bf16))
    x = jnp.concatenate(acts[:inner // LANE], 1)
    b = jnp.concatenate(acts[inner // LANE:(inner + state_dim) // LANE], 1)
    c = jnp.concatenate(acts[(inner + state_dim) // LANE:], 1)

    lane = lax.broadcasted_iota(jnp.int32, (GROUP, LANE), 1)
    real = lane < heads
    v = dot(hidden, w_x[:, mixed:]) + head_par[0:1]
    v_out[...] = v
    dt = jnp.where(real, softplus(v), 0.0)
    tri = triangle(GROUP, False)
    tri_low = tri.astype(f32).astype(bf16)
    cum = fold_lanes(dot(tri_low, split_pack(dt * head_par[1:2], heads)), heads)
    cum = jnp.where(real, cum, 0.0)
    cum_out[...] = cum
    cum_t = cum.T
    _, (dt_wide, ain_wide, end_wide), carry_wide, skip = scan_terms(
        cum, dt, tok, link, head_par[...], spread[...], heads
    )
    x32 = x.astype(f32)
    xdt32 = x32 * dt_wide
    xdt = xdt32.astype(bf16)
    xw = (xdt32 * end_wide).astype(bf16)

    gram = dot(c, b, 1, 1)
    allowed = tri & (tok[:, 0:1] == seg_row)
    off = jnp.where(allowed, 0.0, neg_big)
    first = lane < head_dim
    entering = held[...]
    enter_out[0] = entering
    u = dot(c, entering.astype(bf16))
    zero = jnp.zeros((GROUP, LANE), bf16)
    for pair in range(heads // 2):
        cols = slice(pair * LANE, (pair + 1) * LANE)
        xp = xdt[:, cols]
        intra = 0.0
        for odd in range(2):
            head = 2 * pair + odd
            decay = jnp.exp(cum[:, head:head + 1] - cum_t[head:head + 1] + off)
            weight = (gram * decay).astype(bf16)
            mine = jnp.where(first, xp, zero) if odd == 0 else jnp.where(first, zero, xp)
            intra = intra + dot(weight, mine)
        y_out[:, cols] = intra + ain_wide[:, cols] * u[:, cols] + skip[:, cols] * x32[:, cols]
    held[...] = dot(b, xw, 0, 0) + carry_wide * entering


def gate_forward_kernel(
    meta, hid, y, w_z, w_out, cot0, cot1, cot2, cot3, gate_gain, z_out, dyn_out, cot_out, rows_out
):
    me = meta[0]
    per = cot0.shape[1] // LANE
    z = dot(hid[...], w_z[...])
    z_out[...] = z
    dyn = 0.0
    for rel, cot in enumerate((cot0, cot1, cot2, cot3)):
        absolute = jnp.bitwise_xor(me, rel)
        places = [meta[1 + absolute * per + half] for half in range(per)]
        weight = jnp.concatenate([w_out[block_slice(place), :] for place in places], 0)
        cv = cot[...]
        dyn = dyn + dot(cv, weight)
        for half, place in enumerate(places):
            cot_out[:, block_slice(place)] = cv[:, half * LANE:(half + 1) * LANE]
    dyn_out[...] = dyn
    square = jnp.zeros((z.shape[0], LANE), f32)
    gd = jnp.zeros((z.shape[0], LANE), f32)
    for start in range(0, z.shape[1], LANE):
        cols = slice(start, start + LANE)
        zc = z[:, cols]
        gated = y[:, cols] * zc * sigmoid(zc)
        square = square + gated * gated
        gd = gd + dyn[:, cols] * gate_gain[:, cols] * gated
    square = jnp.sum(square, -1, keepdims=True)
    gd = jnp.sum(gd, -1, keepdims=True)
    upper = lax.broadcasted_iota(jnp.int32, (SUB, GROUP), 0) < SUB // 2
    for i in range(rows_out.shape[0]):
        here = slice(i * GROUP, (i + 1) * GROUP)
        rows_out[i] = jnp.where(upper, to_rows(square[here]), to_rows(gd[here]))


def gate_kernel(
    inner_full,
    meta, sum0, sum1, sum2, sum3, z, y, dyn, w_out, gate_gain, gain_in,
    out0, out1, out2, out3, yn_out, dy_out, dz_out, gain_out,
):
    step = pl.program_id(0)
    me = meta[0]
    both = [
        (sum0[i] + sum1[i] + sum2[i] + sum3[i]).T for i in range(sum0.shape[0])
    ]
    square = jnp.concatenate([columns[:, :1] for columns in both], 0)
    gd = jnp.concatenate([columns[:, SUB - 1:] for columns in both], 0)
    rs = lax.rsqrt(square / inner_full + epsilon)
    inner_dot = gd * rs / inner_full

    @pl.when(step == 0)
    def _():
        gain_out[...] = gain_in[...]

    for start in range(0, z.shape[1], LANE):
        cols = slice(start, start + LANE)
        zc, yc, dc = z[:, cols], y[:, cols], dyn[:, cols]
        sg = sigmoid(zc)
        zs = zc * sg
        gnorm = yc * zs * rs
        yn_out[:, cols] = (gnorm * gate_gain[:, cols]).astype(bf16)
        gain_out[0:1, cols] += jnp.sum(dc * gnorm, 0, keepdims=True)
        dgated = rs * (dc * gate_gain[:, cols] - gnorm * inner_dot)
        dy_out[:, cols] = (dgated * zs).astype(bf16)
        dz_out[:, cols] = (dgated * yc * (sg * (1.0 + zc * (1.0 - sg)))).astype(bf16)
    yn = yn_out[...]
    per = out0.shape[1] // LANE
    for rel, out in enumerate((out0, out1, out2, out3)):
        absolute = jnp.bitwise_xor(me, rel)
        places = [meta[1 + absolute * per + half] for half in range(per)]
        weight = jnp.concatenate([w_out[block_slice(place), :] for place in places], 0)
        out[...] = dot(yn, weight, 1, 1).astype(bf16)


def backward_kernel(
    heads, head_dim, state_dim, last_group, seq, fresh,
    meta, dy_in, dz_in, y, xb_pre, xb_conv, v_in, cum_in, enter_in, hid,
    seg, w_x, w_z, conv_x, conv_bc, head_par, spread, heads_of, sums_in, dheld_in, edge_in,
    dcat, dh0, nd_out, dh1, dh2, dh3, sums, dheld, edge,
    ext1, ext2, ext3,
):
    inner = heads * head_dim
    mixed = inner + 2 * state_dim
    step = pl.program_id(0)
    group = last_group - step
    me = meta[0]

    @pl.when(step == 0)
    def _():
        dheld[...] = jnp.zeros(dheld.shape, f32) if fresh else dheld_in[...]
        edge[...] = jnp.zeros(edge.shape, f32) if fresh else edge_in[...]
        sums[...] = sums_in[...]

    for k, ext in enumerate((ext1, ext2, ext3)):
        ext[GROUP:GROUP + SUB] = edge[k * SUB:(k + 1) * SUB]

    seg_row, tok, link = segment_rows(seg, seq, group)
    dy = dy_in[...]
    dy32 = dy.astype(f32)
    acts, slopes = [], []
    for start in range(0, mixed, LANE):
        conv = xb_conv[:, start:start + LANE]
        sg = sigmoid(conv)
        acts.append((conv * sg).astype(bf16))
        slopes.append(sg * (1.0 + conv * (1.0 - sg)))
    x = jnp.concatenate(acts[:inner // LANE], 1)
    b = jnp.concatenate(acts[inner // LANE:(inner + state_dim) // LANE], 1)
    c = jnp.concatenate(acts[(inner + state_dim) // LANE:], 1)
    x32 = x.astype(f32)

    lane = lax.broadcasted_iota(jnp.int32, (GROUP, LANE), 1)
    real = lane < heads
    v = v_in[...]
    dt = jnp.where(real, softplus(v), 0.0)
    cum = cum_in[...]
    cum_t = cum.T
    w_end, (dt_wide, ain_wide, end_wide), carry_wide, skip = scan_terms(
        cum, dt, tok, link, head_par[...], spread[...], heads
    )
    xdt32 = x32 * dt_wide
    xdt = xdt32.astype(bf16)
    xw = (xdt32 * end_wide).astype(bf16)

    entering = enter_in[0]
    enter_low = entering.astype(bf16)
    dstate = dheld[...]
    dstate_low = dstate.astype(bf16)
    dyw = (dy32 * ain_wide).astype(bf16)
    dc = dot(dyw, enter_low, 1, 1)
    db = dot(xw, dstate_low, 1, 1)
    bd = dot(b, dstate_low)
    gain_sum = jnp.sum(dstate * entering, 0, keepdims=True) * carry_wide
    dheld[...] = dot(c, dyw, 0, 0) + carry_wide * dstate

    gram_t = dot(b, c, 1, 1)
    tri_up = triangle(GROUP, True)
    off = jnp.where(tri_up & (tok[:, 0:1] == seg_row), 0.0, neg_big)
    first = lane < head_dim
    zero = jnp.zeros((GROUP, LANE), bf16)
    dgram_t = jnp.zeros((GROUP, GROUP), f32)
    flow, through = [], []
    for pair in range(heads // 2):
        cols = slice(pair * LANE, (pair + 1) * LANE)
        xp, dyp = xdt[:, cols], dy[:, cols]
        dxw = 0.0
        for odd in range(2):
            head = 2 * pair + odd
            decay = jnp.exp(cum_t[head:head + 1] - cum[:, head:head + 1] + off)
            weight = (gram_t * decay).astype(bf16)
            own_dy = jnp.where(first, dyp, zero) if odd == 0 else jnp.where(first, zero, dyp)
            own_x = jnp.where(first, xp, zero) if odd == 0 else jnp.where(first, zero, xp)
            dxw = dxw + dot(weight, own_dy)
            dgram_t = dgram_t + dot(own_x, dyp, 1, 1) * decay
        x_cols, dy_cols = x32[:, cols], dy32[:, cols]
        ymix = y[:, cols] - skip[:, cols] * x_cols
        flow.append(dy_cols * ymix - xp.astype(f32) * dxw)
        through.append(dxw + end_wide[:, cols] * bd[:, cols])
        sums[0:1, mixed + pair * LANE:mixed + (pair + 1) * LANE] += jnp.sum(
            dy_cols * x_cols, 0, keepdims=True
        )
    dgram_low = dgram_t.astype(bf16)
    db = db + dot(dgram_low, c)
    dc = dc + dot(dgram_low, b, 0, 0)
    q = jnp.concatenate(through, 1)
    flow_sum = head_sums(jnp.concatenate(flow, 1), heads_of[...])
    ddt = head_sums(x32 * q, heads_of[...])
    dv = head_sums(x32 * bd, heads_of[...])
    dw = dv * w_end * dt
    carried = head_sums(jnp.broadcast_to(gain_sum, (SUB, inner)), heads_of[...])[0:1]
    constant = jnp.sum(dw, 0, keepdims=True) + carried
    up = tri_up.astype(f32).astype(bf16)
    inward = jnp.where(real, flow_sum - dw, 0.0)
    dstep = fold_lanes(dot(up, split_pack(inward, heads)), heads) + constant
    dstep = jnp.where(real, dstep, 0.0)
    ddt = ddt + dstep * head_par[1:2]
    dpre = jnp.where(real, ddt * sigmoid(v), 0.0)
    sums[2:3, mixed:mixed + LANE] += jnp.sum(dstep * dt, 0, keepdims=True)
    sums[3:4, mixed:mixed + LANE] += jnp.sum(dpre, 0, keepdims=True)
    dcat[:, mixed:] = dpre.astype(bf16)

    masks = [None] + [jnp.broadcast_to(tok[:, k:k + 1], (GROUP, LANE)) for k in (1, 2, 3)]
    for start in range(0, mixed, LANE):
        cols = slice(start, start + LANE)
        taps = conv_x if start < inner else conv_bc
        own = cols if start < inner else slice(start - inner, start - inner + LANE)
        if start < inner:
            dact = dt_wide[:, cols] * q[:, cols] + skip[:, cols] * dy32[:, cols]
        elif start < inner + state_dim:
            dact = db[:, start - inner:start - inner + LANE]
        else:
            dact = dc[:, start - inner - state_dim:start - inner - state_dim + LANE]
        dconv = dact * slopes[start // LANE]
        pre = xb_pre[:, cols]
        sums[4:5, cols] += jnp.sum(dconv, 0, keepdims=True)
        sums[3:4, cols] += jnp.sum(dconv * pre, 0, keepdims=True)
        dpre_cols = taps[3:4, own] * dconv
        for k, ext in ((1, ext1), (2, ext2), (3, ext3)):
            ext[0:GROUP, cols] = dconv * masks[k]
            shifted = ext[k:k + GROUP, cols]
            dpre_cols = dpre_cols + taps[3 - k:4 - k, own] * shifted
            sums[3 - k:4 - k, cols] += jnp.sum(shifted * pre, 0, keepdims=True)
        dcat[:, cols] = dpre_cols.astype(bf16)
    for k, ext in enumerate((ext1, ext2, ext3)):
        edge[k * SUB:(k + 1) * SUB] = ext[0:SUB]

    grads, dz = dcat[...], dz_in[...]
    per = dh0.shape[1] // LANE
    norm_dot = jnp.zeros((GROUP, LANE), f32)
    norm_rows = jnp.zeros((SUB, LANE), f32)
    row = lax.broadcasted_iota(jnp.int32, (SUB, LANE), 0)
    for rel, dh in enumerate((dh0, dh1, dh2, dh3)):
        absolute = jnp.bitwise_xor(me, rel)
        places = [meta[1 + absolute * per + half] for half in range(per)]
        weight_x = jnp.concatenate([w_x[block_slice(place), :] for place in places], 0)
        weight_z = jnp.concatenate([w_z[block_slice(place), :] for place in places], 0)
        part = dot(grads, weight_x, 1, 1) + dot(dz, weight_z, 1, 1)
        dh[...] = part.astype(bf16)
        for half, place in enumerate(places):
            cols = slice(half * LANE, (half + 1) * LANE)
            product = part[:, cols] * hid[:, block_slice(place)].astype(f32)
            norm_dot = norm_dot + product
            norm_rows = norm_rows + jnp.where(
                row == absolute * per + half, jnp.sum(product, 0, keepdims=True), 0.0
            )
    sums[:, mixed + inner:] += norm_rows
    nd_out[0] = to_rows(jnp.sum(norm_dot, -1, keepdims=True))


def last_kernel(width, counts, meta, gain, rs_row, nd, rows, cot, dh, *refs):
    grad = refs[-1]
    part = rows.shape[1]
    own_gain = gain[:, pl.ds(pl.multiple_of(meta[0] * part, LANE), part)]
    length = refs[0].shape[0]
    starts = [sum(counts[:i]) for i in range(len(counts))]
    for index in range(rs_row.shape[0]):
        here = slice(index * GROUP, (index + 1) * GROUP)
        quarter, inside = divmod(index * GROUP, length)
        there = slice(inside, inside + GROUP)
        rs = to_column(rs_row[index])
        mean = to_column(nd[index]) / width
        normed = rows[here].astype(f32) * rs
        total = dh[here].astype(f32)
        for piece in refs[starts[quarter]:starts[quarter] + counts[quarter]]:
            total = total + piece[there].astype(f32)
        grad[here] = (cot[here].astype(f32) + rs * (total * own_gain - normed * mean)).astype(bf16)


def smem():
    return pl.BlockSpec(memory_space=pltpu.SMEM)


def whole(array):
    zeros = (0,) * array.ndim
    return pl.BlockSpec(array.shape, lambda i: zeros)


def run(kernel, steps, ins, outs, scratch, flops, bytes_accessed, kept=None):
    kept = kept or {}
    unread = len(kept)

    def body(*refs):
        kernel(*refs[unread:])

    return pl.pallas_call(
        body,
        grid=(steps,),
        in_specs=[pl.BlockSpec(memory_space=pl.ANY)] * unread + [spec for _, spec in ins],
        out_specs=[spec for _, spec in outs],
        out_shape=[shape for shape, _ in outs],
        scratch_shapes=scratch,
        input_output_aliases={i: place for i, place in enumerate(kept)},
        compiler_params=pltpu.CompilerParams(
            vmem_limit_bytes=VMEM_LIMIT, dimension_semantics=("arbitrary",)
        ),
        cost_estimate=pl.CostEstimate(
            flops=flops, bytes_accessed=bytes_accessed, transcendentals=0
        ),
    )(*kept.values(), *[array for array, _ in ins])


def ring_order(count):
    return list(range(0, count, 2)) + list(range(count - 1 - count % 2, 0, -2))


def ring_pairs(count, shift):
    order = ring_order(count)
    return [(order[i], order[(i + shift) % count]) for i in range(count)]


def swap(array, axis, rel):
    count = lax.axis_size(axis)
    return lax.ppermute(array, axis, [(i, i ^ rel) for i in range(count)])


def ring_hand_on(blocks, step, ends):
    count = len(blocks)
    ahead, back = ends
    ahead = blocks[step] = lax.ppermute(ahead, "fsdp", ring_pairs(count, 1))
    if step < count - step:
        back = blocks[count - step] = lax.ppermute(back, "fsdp", ring_pairs(count, -1))
    return ahead, back


def ring_distance(step):
    count = lax.axis_size("fsdp")
    return {1: count // 2 - step, -1: count - 1 - count // 2 - step}


def ring_first(blocks):
    return {
        shift: blocks[(-shift * far) % len(blocks)]
        for shift, far in ring_distance(0).items() if far > 0
    }


def ring_move(blocks, step, moving, waits=()):
    onward, arrived = {}, []
    for shift, far in ring_distance(step).items():
        if far <= 0:
            continue
        got = lax.ppermute(moving[shift], "fsdp", ring_pairs(len(blocks), shift))
        if far == 1:
            arrived.append(got)
        else:
            mine = blocks[(-shift * (far - 1)) % len(blocks)]
            if waits:
                (mine,) = after((mine,), waits)
            onward[shift] = (mine.astype(f32) + got.astype(f32)).astype(bf16)
    return onward, arrived


def double_up(array, axis):
    rel = 1
    while rel < lax.axis_size(axis):
        array = array + swap(array, axis, rel)
        rel *= 2
    return array


def head_gather(own):
    far = swap(own, "head", 2)
    return [own, swap(own, "head", 1), far, swap(far, "head", 1)]


def spread_rows(rows):
    return [rows] + [swap(rows, "head", rel) for rel in (1, 2, 3)]


def after(arrays, others):
    return lax.optimization_barrier((tuple(arrays), tuple(others)))[0]


def shards(
    block_in, segment_ids, norm_gain, proj_z, proj_x, proj_bc, proj_dt, conv_x, bias_x, conv_bc,
    bias_bc, dt_bias, a_log, skip_d, gate_gain, proj_out, cotangent,
):
    seqs, seq_len = segment_ids.shape
    tokens = seqs * seq_len
    head_devs = lax.axis_size("head")
    fsdp_devs = lax.axis_size("fsdp")
    me = lax.axis_index("head")
    width_part = block_in.shape[1]
    width = width_part * head_devs
    heads = dt_bias.shape[0]
    inner = bias_x.shape[0]
    head_dim = inner // heads
    inner_full = inner * head_devs
    state_dim = conv_bc.shape[1] // 2
    mixed = inner + 2 * state_dim
    n_groups = seq_len // GROUP
    groups = seqs * n_groups
    feature_blocks = width // LANE
    ringed = fsdp_devs == feature_blocks
    back_cols = mixed + LANE

    join_ins = (proj_z, proj_out, proj_x, proj_bc, proj_dt.T)
    late_mine, early_mine = pl.pallas_call(
        functools.partial(join_kernel, LANE),
        out_shape=[
            jax.ShapeDtypeStruct((proj_z.shape[0], 2 * inner), bf16),
            jax.ShapeDtypeStruct((proj_z.shape[0], back_cols), bf16),
        ],
    )(*join_ins)
    rows_all = head_gather(block_in)
    late_blocks = [late_mine] + [None] * (fsdp_devs - 1)
    if ringed:
        order = ring_order(fsdp_devs)
        position = np.array([order.index(i) for i in range(fsdp_devs)])
        places = (position[:, None] - position[None]) % fsdp_devs
        early_blocks = [early_mine] + [None] * (fsdp_devs - 1)
        ends = (early_mine, early_mine)
        for step in range(1, fsdp_devs // 2 + 1):
            ends = ring_hand_on(early_blocks, step, ends)
        w_x = jnp.concatenate(early_blocks, 0)
        (cot_mine,) = after((cotangent,), (rows_all[2],))
        cot_far = swap(cot_mine, "head", 2)
    else:
        cot_far = swap(cotangent, "head", 2)
        places = np.tile(np.arange(feature_blocks), (fsdp_devs, 1))
        w_x, w_zo = [
            lax.all_gather(a, "fsdp", axis=0, tiled=True) for a in (early_mine, late_mine)
        ]
    table = np.zeros((fsdp_devs, head_devs, 1 + feature_blocks), np.int32)
    table[:, :, 0] = np.arange(head_devs)[None]
    table[:, :, 1:] = places[:, None]
    meta = lax.dynamic_index_in_dim(
        jnp.asarray(table.reshape(-1, 1 + feature_blocks)),
        lax.axis_index(("fsdp", "head")), 0, False,
    )

    head_par = jnp.pad(
        jnp.stack([dt_bias, -jnp.exp(a_log), skip_d]), ((0, SUB - 3), (0, LANE - heads))
    )
    lanes = np.arange(LANE)[:, None]
    owners = (np.arange(inner) // head_dim)[None]
    spread = jnp.asarray(((lanes % heads == owners) & (lanes < 3 * heads)), bf16)
    heads_of = jnp.asarray((lanes == owners).T, bf16)
    gain = norm_gain[None]
    gate_row = gate_gain[None]

    token_shape = lambda cols, dtype: jax.ShapeDtypeStruct((tokens, cols), dtype)
    row_shape = lambda count: jax.ShapeDtypeStruct((count, SUB, GROUP), f32)

    def keep(earlier, count):
        return {i: earlier[i] for i in range(count)} if earlier else {}

    enter_shape = jax.ShapeDtypeStruct((groups, state_dim, inner), f32)

    wide = 2 if n_groups % 2 == 0 else 1
    quarter = wide
    quarter_rows = quarter * GROUP
    per_seq = n_groups // quarter
    state_shape = jax.ShapeDtypeStruct((state_dim, inner), f32)

    def z_weights(side):
        return (w_zo, pl.BlockSpec((width, inner), lambda i: (0, side)))

    def forward(s, q, earlier, waits):
        base = s * n_groups + q * quarter
        part = lambda cols: pl.BlockSpec((GROUP, cols), lambda i: (base + i, 0))
        row = lambda rows, cols: pl.BlockSpec((1, rows, cols), lambda i: (base + i, 0, 0))
        edge_shape = jax.ShapeDtypeStruct((SUB, mixed), f32)
        state, edge = (earlier[8], earlier[9]) if earlier else (
            jnp.zeros(state_shape.shape, f32), jnp.zeros(edge_shape.shape, f32)
        )
        (state,) = after((state,), waits)
        ins = [(meta, smem())] + [(r, part(width_part)) for r in rows_all]
        consts = (
            segment_ids, w_x, gain, conv_x, conv_bc, bias_x[None], bias_bc[None], head_par, spread,
            state, edge,
        )
        ins += [(a, whole(a)) for a in consts]
        outs = [(token_shape(width, bf16), part(width))]
        outs += [
            (token_shape(cols, f32), part(cols)) for cols in (mixed, mixed, LANE, LANE, inner)
        ]
        outs += [(enter_shape, row(state_dim, inner)), (row_shape(groups), row(SUB, GROUP))]
        outs += [(a, whole(a)) for a in (state_shape, edge_shape)]
        scratch = [pltpu.VMEM((GROUP + SUB, mixed), f32)]
        kernel = functools.partial(
            forward_kernel, heads, head_dim, state_dim, q * quarter, s, q == 0
        )
        return run(
            kernel, quarter, ins, outs, scratch, 16 * 10**9, 10 * 2**20, keep(earlier, 8)
        )

    def tall(cols, base=0):
        return pl.BlockSpec((wide * GROUP, cols), lambda i: (base // wide + i, 0))

    def tall_row(base=0):
        return pl.BlockSpec((wide, SUB, GROUP), lambda i: (base // wide + i, 0, 0))

    def gate_forward(s, hid, y, earlier):
        base = s * n_groups
        ins = [(meta, smem()), (hid, tall(width, base)), (y, tall(inner, base))]
        ins += [z_weights(0), z_weights(1)]
        ins += [(c, tall(width_part, base)) for c in cots] + [(gate_row, whole(gate_row))]
        outs = [(token_shape(inner, f32), tall(inner, base))] * 2
        outs += [(token_shape(width, bf16), tall(width, base)), (row_shape(n_groups), tall_row())]
        return run(
            gate_forward_kernel, n_groups // wide, ins, outs, [], 8 * 10**9, 12 * 2**20,
            keep(earlier, 3),
        )

    def gate(s, totals, z, y, dyn, gain_in, earlier):
        base = s * n_groups
        ins = [(meta, smem())] + [(a, tall_row()) for a in totals]
        ins += [(a, tall(inner, base)) for a in (z, y, dyn)]
        ins += [z_weights(1)] + [(a, whole(a)) for a in (gate_row, gain_in)]
        gain_shape = jax.ShapeDtypeStruct((SUB, inner), f32)
        outs = [(token_shape(width_part, bf16), tall(width_part, base))] * 4
        outs += [(token_shape(inner, bf16), tall(inner, base))] * 3
        outs += [(gain_shape, whole(gain_shape))]
        kernel = functools.partial(gate_kernel, inner_full)
        return run(kernel, n_groups // wide, ins, outs, [], 10 * 10**9, 12 * 2**20, keep(earlier, 7))

    def backward(s, q, arrays, enter, hid, sums_in, earlier, waits):
        base = s * n_groups + q * quarter
        fresh = (q + 1) * quarter == n_groups

        def back_part(cols, first=base):
            return pl.BlockSpec((GROUP, cols), lambda i: (first + quarter - 1 - i, 0))

        def back_row(rows=SUB, cols=GROUP):
            return pl.BlockSpec((1, rows, cols), lambda i: (base + quarter - 1 - i, 0, 0))

        edge_shape = jax.ShapeDtypeStruct((3 * SUB, mixed), f32)
        sums_shape = jax.ShapeDtypeStruct(sums_in.shape, f32)
        state, edge = (earlier[7], earlier[8]) if earlier else (
            jnp.zeros(state_shape.shape, f32), jnp.zeros(edge_shape.shape, f32)
        )
        ins = [(meta, smem())] + [(a, back_part(a.shape[1])) for a in arrays]
        ins += [(enter, back_row(state_dim, inner)), (hid, back_part(width))]
        ins += [(segment_ids, whole(segment_ids)), (w_x, whole(w_x)), z_weights(0)]
        (sums_in,) = after((sums_in,), waits)
        consts = (conv_x, conv_bc, head_par, spread, heads_of, sums_in, state, edge)
        ins += [(a, whole(a)) for a in consts]
        dh_shape = jax.ShapeDtypeStruct((quarter_rows, width_part), bf16)
        outs = [(token_shape(back_cols, bf16), back_part(back_cols))]
        outs += [(token_shape(width_part, bf16), back_part(width_part))]
        outs += [(row_shape(groups), back_row())]
        outs += [(dh_shape, back_part(width_part, 0))] * 3
        outs += [(a, whole(a)) for a in (sums_shape, state_shape, edge_shape)]
        scratch = [pltpu.VMEM((GROUP + SUB, mixed), f32)] * 3
        kernel = functools.partial(
            backward_kernel, heads, head_dim, state_dim, (q + 1) * quarter - 1, s, fresh
        )
        return run(
            kernel, quarter, ins, outs, scratch, 30 * 10**9, 13 * 2**20, keep(earlier, 3)
        )

    def last(nears, fars, dots, dh):
        pieces = [[near, *(far if isinstance(far, list) else [far])] for near, far in zip(nears, fars)]
        arrays = [meta, gain, norm_rs, *dots, block_in, cotangent, dh, *sum(pieces, [])]
        ins = [(a, whole(a)) for a in arrays]
        ins[0] = (meta, smem())
        shape = token_shape(width_part, bf16)
        counts = tuple(len(piece) for piece in pieces)
        kernel = functools.partial(last_kernel, width, counts)
        return run(kernel, 1, ins, [(shape, whole(shape))], [], 4 * 10**9, 8 * 2**20)[0]

    def far_sum(mine, got):
        return (mine.astype(f32) + got.astype(f32)).astype(bf16)

    fwd = None
    steps = [(s, q) for s in range(seqs) for q in range(per_seq)]
    ends = (late_mine, late_mine)
    if ringed:
        ends = after(ends, (w_x,))
    for index, (s, q) in enumerate(steps):
        waits = tuple(ends) if ringed else ()
        if ringed and index < fsdp_devs // 2:
            ends = ring_hand_on(late_blocks, index + 1, ends)
        fwd = forward(s, q, fwd, waits)
        if ringed:
            ends = after(ends, (fwd[8],))
        if index == len(steps) // 2:
            near_cot, far_cot = after((cotangent, cot_far), (fwd[8],))
            cots = [cotangent, swap(near_cot, "head", 1), cot_far, swap(far_cot, "head", 1)]
    hid, xb_pre, xb_conv, v, cum, y, enter, norm_rs = fwd[:8]
    if ringed:
        w_zo = jnp.concatenate(late_blocks, 0)
    gate_fwd, totals = None, []
    for s in range(seqs):
        gate_fwd = gate_forward(s, hid, y, gate_fwd)
        totals.append(spread_rows(gate_fwd[3]))
    z, dyn, cot_whole = gate_fwd[:3]
    gates, gain_sum = None, jnp.zeros((SUB, inner), f32)
    for s in range(seqs):
        gates = gate(s, totals[s], z, y, dyn, gain_sum, gates)
        gain_sum = gates[7]
    out0, out1, out2, out3, yn, dy, dz = gates[:7]
    got1, got3 = swap(out1, "head", 1), swap(out3, "head", 1)
    g_out = dot(cot_whole, yn, 0, 0).astype(bf16)
    out_sum = far_sum(*after((out2, got3), (got1,)))
    out_far = swap(out_sum, "head", 2)
    out_rows = (
        block_in.astype(f32) + out0.astype(f32) + got1.astype(f32) + out_far.astype(f32)
    ).astype(bf16)
    g_z = dot(hid, dz, 0, 0).astype(bf16)
    g_early = jnp.concatenate([g_z, g_out], 1)
    (g_early,) = after((g_early,), (out_sum,))
    blocks = lambda a: [a[i * LANE:(i + 1) * LANE] for i in range(feature_blocks)]
    scatter = lambda a: lax.psum_scatter(
        a.astype(f32), "fsdp", scatter_dimension=0, tiled=True
    )
    moving = ring_first(blocks(g_early)) if ringed else {}
    arrived = []

    sums = jnp.pad(gain_sum[:1], ((1, SUB - 2), (mixed, LANE)))
    steps = [(s, q) for s in range(seqs) for q in reversed(range(per_seq))]
    back = None
    nears, far_gots, pair = [], [], None
    for index, (s, q) in enumerate(steps):
        waits = [g_early, out_sum, *moving.values(), *nears[:max(index - 1, 0)]]
        waits += far_gots[:max(index - 2, 0)]
        if index >= 2:
            waits.append(out_rows)
        back = backward(
            s, q, (dy, dz, y, xb_pre, xb_conv, v, cum), enter, hid, sums, back, waits
        )
        _, dh0, nd, dh1, dh2, dh3, sums = back[:7]
        if pair:
            far = far_sum(*after(pair, (sums,)))
            far_gots.append(swap(far, "head", 2))
        if moving:
            moving, got = ring_move(blocks(g_early), index, moving, (sums,))
            arrived += got
        nears.append(swap(dh1, "head", 1))
        pair = None
        if index + 1 < len(steps):
            pair = (dh2, swap(dh3, "head", 1))
    far_gots.append([swap(dh2, "head", 2), swap(dh3, "head", 3)])
    (dcat,) = after((back[0],), (*nears[:-1], *far_gots[:-2], *arrived, far))
    g_late = dot(hid, dcat, 0, 0).astype(bf16)
    places_of = {s * per_seq + q: i for i, (s, q) in enumerate(steps)}
    near_at = [nears[places_of[i]] for i in range(len(steps))]
    far_at = [far_gots[places_of[i]] for i in range(len(steps))]

    def finish(dots):
        return last(near_at, far_at, dots, back[1])

    if ringed:
        s_early = sum([a.astype(f32) for a in arrived], g_early[:LANE].astype(f32))
        moving = ring_first(blocks(g_late))
        s_late = g_late[:LANE].astype(f32)
        for step in range(fsdp_devs // 2):
            moving, got = ring_move(blocks(g_late), step, moving)
            s_late = sum([a.astype(f32) for a in got], s_late)
            if step == 0:
                nd, sums = after((nd, sums), tuple(moving.values()))
                dots = (double_up(nd, "head"),)
            if step == min(1, fsdp_devs // 2 - 1):
                pieces = (*dots, far_gots[-2], nears[-1])
                grad_rows = finish(dots)
                if moving:
                    moving = dict(zip(moving, after(moving.values(), pieces)))
            if step == 2 and moving:
                moving = dict(zip(moving, after(moving.values(), (grad_rows,))))
    else:
        s_early, s_late = scatter(g_early), scatter(g_late)
        grad_rows = finish((double_up(nd, "head"),))
    bc_part = 2 * state_dim // head_devs
    s_bc_all = s_late[:, inner:mixed].reshape(-1, head_devs, bc_part).transpose(1, 0, 2)
    s_bc = lax.dynamic_index_in_dim(s_bc_all, me, 0, False)
    for rel in (1, 2, 3):
        s_bc = s_bc + swap(lax.dynamic_index_in_dim(s_bc_all, me ^ rel, 0, False), "head", rel)

    fsdp_sums = double_up(sums, "fsdp")
    all_sums = double_up(fsdp_sums, "head")
    norm_sums = all_sums[:, mixed + inner:].reshape(head_devs, width_part) / norm_gain.reshape(
        head_devs, width_part
    )
    return (
        out_rows,
        grad_rows,
        lax.dynamic_index_in_dim(norm_sums, me, 0, False),
        s_early[:, :inner],
        s_late[:, :inner],
        s_bc,
        s_late[:, mixed:mixed + heads],
        fsdp_sums[:4, :inner],
        fsdp_sums[4, :inner],
        all_sums[:4, inner:mixed],
        all_sums[4, inner:mixed],
        fsdp_sums[3, mixed:mixed + heads],
        fsdp_sums[2, mixed:mixed + heads] * -jnp.exp(a_log),
        fsdp_sums[0, mixed:mixed + inner].reshape(heads, head_dim).sum(1),
        fsdp_sums[1, mixed:mixed + inner],
        s_early[:, inner:].T,
    )


def solution(mesh):
    in_specs = (
        P("fsdp", "head"), P("fsdp", None), P(), P("fsdp", "head"), P("fsdp", "head"),
        P("fsdp", None), P("fsdp", "head"), P(None, "head"), P("head"), P(), P(), P("head"),
        P("head"), P("head"), P("head"), P("head", "fsdp"), P("fsdp", "head"),
    )
    out_specs = (
        P("fsdp", "head"), P("fsdp", "head"), P("head"), P("fsdp", "head"), P("fsdp", "head"),
        P("fsdp", "head"), P("fsdp", "head"), P(None, "head"), P("head"), P(), P(), P("head"),
        P("head"), P("head"), P("head"), P("head", "fsdp"),
    )
    return jax.shard_map(shards, mesh=mesh, in_specs=in_specs, out_specs=out_specs, check_vma=False)
```
